512 devices in a mesh: dp: 4 (over y), row: 8 (over z_lo, core), col: 16 (over z_hi, x).
Axes of the slice: x: 4, y: 4, z: 16 (z_hi: 4, z_lo: 4; z = z_hi * 4 + z_lo), core: 2. Of those that a mesh axis runs over, the one named last changes fastest.
Arguments:
- gradient_partials: bfloat16 [4, 4, 1024, 16384], P('dp', None, 'row', 'col'), may hold values from -405 to 405
- master: float32 [4, 1024, 16384], P('dp', 'row', 'col'), may hold values from -0.03 to 0.03
- row_moment: float32 [4, 1024], P('dp', 'row'), may hold values from 0.5 to 50
- col_moment: float32 [16384], P('col'), may hold values from 0.5 to 50
- amax_history: float32 [16], replicated, may hold values from 0.03 to 0.08
Outputs:
- new_master: float32 [4, 1024, 16384], P('dp', 'row', 'col')
- update: float32 [4, 1024, 16384], P('dp', 'row', 'col')
- row_new: float32 [4, 1024], P('dp', 'row')
- col_new: float32 [16384], P('col')
- codes: bfloat16 [4, 1024, 16384], P(None, 'row', 'col')
- new_history: float32 [16], replicated
- row_mean: float32 [], replicated
The draws below stay inside these ranges and needn't reach their ends.
All inputs are finite; a program needn't handle non-finite values.
Results may differ from the reference program's by a relative error of at most 0.012.
Values may be sent and summed in bfloat16 or wider, within the bound.
A program may use at most 64 MiB of HBM per device.

```python
import math
import jax
import jax.numpy as jnp
from jax import lax

D_WIN = 4096
FF_WIN = 16384
HIST = 16
N_DP = 4


def draw_gradient_partials(key, part):
    key = jax.random.fold_in(key, 7)
    key_rows, key_cols, key_own = jax.random.split(key, 3)
    block_rows = D_WIN // N_DP
    shape = (N_DP, N_DP, block_rows, FF_WIN)
    position = jnp.arange(D_WIN, dtype=jnp.float32).reshape(N_DP, block_rows) / D_WIN
    row_scale = jnp.exp(jax.random.uniform(key_rows, (N_DP, block_rows), jnp.float32, math.log(0.3), math.log(3.0))) * jnp.exp(math.log(3.0) * position)
    col_position = jnp.arange(FF_WIN, dtype=jnp.float32) / FF_WIN
    col_scale = jnp.exp(jax.random.uniform(key_cols, (FF_WIN,), jnp.float32, math.log(0.3), math.log(3.0))) * jnp.exp(math.log(3.0) * col_position)
    base = jnp.clip(jax.random.normal(key_own, shape, jnp.float32), -5.0, 5.0)
    values = base * row_scale[None, :, :, None] * col_scale[None, None, None, :]
    return values.astype(jnp.bfloat16)


def level_of(rng, dims, pieces, smallest, largest):
    factor_of = 1.0
    for dim, blocks in pieces:
        steps = jax.random.uniform(jax.random.fold_in(jax.random.fold_in(rng, 6), dim), (blocks,), jnp.float32, smallest / len(pieces), largest / len(pieces))
        factor_of = factor_of * jnp.repeat(jnp.exp(steps), dims[dim] // blocks).reshape((-1,) + (1,) * (len(dims) - 1 - dim))
    return factor_of


def setup_inputs(seed: int = 0) -> dict:
    key_of = jax.random.split(jax.random.key(seed), 6)
    return {
        "gradient_partials": draw_gradient_partials(jax.random.fold_in(key_of[5], 71), 0),
        "master": jnp.clip(jax.random.uniform(key_of[1], (N_DP, D_WIN // N_DP, FF_WIN), jnp.float32, -0.03, 0.03) * level_of(key_of[1], (N_DP, D_WIN // N_DP, FF_WIN), ((0, 4), (1, 8), (2, 16)), -0.4, 0.0), -0.03, 0.03),
        "row_moment": jnp.clip(jnp.exp(math.log(50.0) - 4.6051702 * jax.random.uniform(key_of[2], (N_DP, D_WIN // N_DP), jnp.float32) ** level_of(key_of[2], (N_DP, D_WIN // N_DP), ((0, 4), (1, 8)), -0.2, 0.2)), 0.5, 50.0),
        "col_moment": jnp.clip(jnp.exp(math.log(50.0) - 4.6051702 * jax.random.uniform(key_of[3], (FF_WIN,), jnp.float32) ** level_of(key_of[3], (FF_WIN,), ((0, 16),), -0.2, 0.2)), 0.5, 50.0),
        "amax_history": jnp.clip(jnp.exp(jax.random.uniform(key_of[4], (HIST,), jnp.float32, math.log(0.03), math.log(0.08))), 0.03, 0.08),
    }


decay_rate = 0.9
epsilon = 1e-30
learn_rate = 0.01
clip_limit = 1.0
code_limit = 4.0

def reference(gradient_partials, master, row_moment, col_moment, amax_history):
    gradient = gradient_partials[0].astype(jnp.float32)
    for replica in range(1, N_DP):
        gradient = gradient + gradient_partials[replica].astype(jnp.float32)
    square = gradient * gradient + epsilon
    row_new = decay_rate * row_moment + (1.0 - decay_rate) * lax.optimization_barrier(jnp.mean(square, axis=2))
    col_new = decay_rate * col_moment + (1.0 - decay_rate) * lax.optimization_barrier(jnp.mean(square, axis=(0, 1)))
    row_mean = jnp.mean(row_new)
    denominator = jnp.sqrt(row_new[:, :, None] * col_new[None, None, :] / row_mean)
    raw_step = gradient / denominator
    step_rms = jnp.sqrt(jnp.mean(raw_step * raw_step))
    update = raw_step / jnp.maximum(1.0, step_rms / clip_limit)
    new_master = master - learn_rate * update
    scale = code_limit / jnp.max(amax_history)
    codes = jnp.clip(new_master * scale, -code_limit, code_limit).astype(jnp.bfloat16)
    newest = jnp.max(jnp.abs(new_master))
    new_history = jnp.concatenate([amax_history[1:], newest.reshape(1).astype(jnp.float32)])
    return (new_master, update, row_new, col_new, codes, new_history, row_mean.astype(jnp.float32))
```

```python
import functools

import jax
import jax.numpy as jnp
from jax import lax
from jax.experimental import pallas as pl
from jax.experimental.pallas import tpu as pltpu
from jax.sharding import PartitionSpec as P

MESH = pl.DeviceIdType.MESH
F32 = jnp.float32

decay_rate = 0.9
epsilon = 1e-30
learn_rate = 0.01
clip_limit = 1.0
code_limit = 4.0

ROWS, COLS = 128, 1024
HALF = ROWS // 2
CHUNK = 32
TILES = COLS // 128


def whole_wait(view, sem):
    pltpu.make_async_copy(view, view, sem).wait()


def step_kernel(
    sizes, grad, master, row_prev, col_prev, history,
    nm_out, up_out, codes_out, small_out,
    merge_r, merge_l, from_l, from_r, own, next_own, prev_own, sum_r, sum_l,
    g_buf, m_buf, nm_buf, up_buf, code_buf, rowp, rm_buf, cm_buf,
    core_c, yz_c, xz_r, xz_t, core_s, yz_s, xz_m, core_m, yz_m,
    rs_send, rs_recv, loc, core_send, core_recv, grp_send, grp_recv, ag_send, ag_recv,
):
    n_dp, n_row, n_col = sizes
    n_zl = n_row // 2
    n_yz = n_dp * n_zl
    total_rows, total_cols = n_dp * n_row * ROWS, n_col * COLS
    d, r, c = lax.axis_index("dp"), lax.axis_index("row"), lax.axis_index("col")
    zl, core = r // 2, r % 2
    q = d * n_zl + zl
    dn, dp_, do = lax.rem(d + 1, n_dp), lax.rem(d + n_dp - 1, n_dp), lax.rem(d + 2, n_dp)
    right, left = (dn, r, c), (dp_, r, c)
    mate = (d, zl * 2 + (1 - core), c)
    yz_peers = []
    for k in range(1, n_yz):
        p = lax.rem(q + k, n_yz)
        yz_peers.append((p // n_zl, (p % n_zl) * 2 + core, c))
    xz_peers = [(d, r, lax.rem(c + k, n_col)) for k in range(1, n_col)]
    contacts = [*yz_peers, mate, *xz_peers]

    def remote(src, dst, send, recv, to):
        return pltpu.make_async_remote_copy(
            src, dst, send, recv, device_id=to, device_id_type=MESH
        )

    loads = [
        pltpu.make_async_copy(grad.at[0, d], own, loc.at[0]),
        pltpu.make_async_copy(grad.at[0, dn, pl.ds(0, HALF)], next_own, loc.at[1]),
        pltpu.make_async_copy(grad.at[0, dp_, pl.ds(HALF, HALF)], prev_own, loc.at[2]),
        pltpu.make_async_copy(master.at[0], m_buf, loc.at[3]),
        pltpu.make_async_copy(row_prev, rm_buf, loc.at[4]),
        pltpu.make_async_copy(col_prev, cm_buf, loc.at[5]),
    ]

    barrier = pltpu.get_barrier_semaphore()
    for p in contacts:
        pl.semaphore_signal(barrier, inc=1, device_id=p, device_id_type=MESH)
    for cp in loads:
        cp.start()
    pl.semaphore_wait(barrier, len(contacts))

    n_half = HALF // CHUNK
    sends = []
    first = []
    for i in range(n_half):
        lo, hi = pl.ds(CHUNK * i, CHUNK), pl.ds(HALF + CHUNK * i, CHUNK)
        here = pl.ds(CHUNK * i, CHUNK)
        a = remote(grad.at[0, do, lo], merge_r.at[here], rs_send.at[i], rs_recv.at[i], right)
        b = remote(grad.at[0, do, hi], merge_l.at[here], rs_send.at[2 + i], rs_recv.at[2 + i], left)
        a.start()
        b.start()
        first.append((a, b))
    plain_r = remote(
        grad.at[0, dn, pl.ds(HALF, HALF)], from_l.at[pl.ds(HALF, HALF)], rs_send.at[4], rs_recv.at[4], right
    )
    plain_l = remote(
        grad.at[0, dp_, pl.ds(0, HALF)], from_r.at[pl.ds(0, HALF)], rs_send.at[5], rs_recv.at[5], left
    )
    plain_r.start()
    plain_l.start()
    loads[1].wait()
    loads[2].wait()
    merged = []
    for i in range(n_half):
        here, hi = pl.ds(CHUNK * i, CHUNK), pl.ds(HALF + CHUNK * i, CHUNK)
        a, b = first[i]
        a.wait_recv()
        sum_r[here] = (next_own[here].astype(F32) + merge_r[here].astype(F32)).astype(jnp.bfloat16)
        m = remote(sum_r.at[here], from_l.at[here], rs_send.at[6 + i], rs_recv.at[6 + i], right)
        m.start()
        b.wait_recv()
        sum_l[here] = (prev_own[here].astype(F32) + merge_l[here].astype(F32)).astype(jnp.bfloat16)
        n = remote(sum_l.at[here], from_r.at[hi], rs_send.at[8 + i], rs_recv.at[8 + i], left)
        n.start()
        merged.append((m, n))

    loads[0].wait()
    plain_r.wait_recv()
    plain_l.wait_recv()
    col_sum = jnp.zeros((8, COLS), F32)
    for i in range(n_half):
        m, n = merged[i]
        for half, cp in ((0, m), (1, n)):
            cp.wait_recv()
            rows = pl.ds(HALF * half + CHUNK * i, CHUNK)
            g = own[rows].astype(F32) + from_l[rows].astype(F32) + from_r[rows].astype(F32)
            g_buf[rows] = g
            square = g * g + epsilon
            for j in range(CHUNK // 8):
                col_sum = col_sum + square[8 * j : 8 * j + 8]
            lanes = square[:, 0:128]
            for k in range(1, TILES):
                lanes = lanes + square[:, 128 * k : 128 * k + 128]
            rowp[rows] = lanes

    flat = jnp.sum(col_sum, axis=0, keepdims=True)
    packed = jnp.concatenate([flat[:, 128 * k : 128 * k + 128] for k in range(TILES)], axis=0)
    core_c[0] = packed
    core_c_copy = remote(core_c.at[0], core_c.at[1], core_send.at[0], core_recv.at[0], mate)
    core_c_copy.start()

    def group_start(buf, mine, peers, i):
        for p in peers:
            remote(buf.at[mine], buf.at[mine], grp_send.at[i], grp_recv.at[i], p).start()

    def group_wait(buf, peers, i):
        whole_wait(buf.at[pl.ds(0, len(peers))], grp_recv.at[i])

    def group_done(buf, peers, i):
        whole_wait(buf.at[pl.ds(0, len(peers))], grp_send.at[i])

    def add_all(buf, n):
        total = buf[0]
        for k in range(1, n):
            total = total + buf[k]
        return total

    def lanes_to_row(values):
        return jnp.sum(values.T, axis=0, keepdims=True)

    def row_to_lanes(values):
        return jnp.broadcast_to(values, (128, 128)).T

    xz_r[c] = lanes_to_row(rowp[...])
    group_start(xz_r, c, xz_peers, 0)
    core_c_copy.wait_recv()
    yz_c[q] = core_c[0] + core_c[1]
    group_start(yz_c, q, yz_peers, 1)
    loads[4].wait()
    loads[5].wait()
    group_wait(yz_c, yz_peers, 1)
    col_total = add_all(yz_c, n_yz)
    col_old = jnp.concatenate(
        [cm_buf[pl.ds(128 * k, 128)].reshape(1, 128) for k in range(TILES)], axis=0
    )
    col_new = decay_rate * col_old + (1.0 - decay_rate) * (col_total / total_rows)
    small_out[0:8] = col_new
    inv_col = 1.0 / col_new
    root_col = 1.0 / jnp.sqrt(col_new)

    lanes = jnp.zeros((ROWS, 128), F32)
    for k in range(TILES):
        g = g_buf[:, pl.ds(128 * k, 128)]
        lanes = lanes + g * g * inv_col[k : k + 1]
    xz_t[c] = lanes_to_row(lanes)
    group_start(xz_t, c, xz_peers, 2)
    group_wait(xz_r, xz_peers, 0)
    row_total = add_all(xz_r, n_col)
    row_new = decay_rate * rm_buf[...] + (1.0 - decay_rate) * (row_total / total_cols)
    small_out[8:9] = row_new
    row_factor = row_to_lanes(1.0 / jnp.sqrt(row_new))
    group_wait(xz_t, xz_peers, 2)
    weighted = add_all(xz_t, n_col) / row_new

    core_s[0] = jnp.concatenate([weighted, row_new], axis=0)
    core_s_copy = remote(core_s.at[0], core_s.at[1], core_send.at[1], core_recv.at[1], mate)
    core_s_copy.start()
    core_s_copy.wait_recv()
    yz_s[q] = core_s[0] + core_s[1]
    group_start(yz_s, q, yz_peers, 3)
    largest_old = history[0]
    for i in range(1, 16):
        largest_old = jnp.maximum(largest_old, history[i])
    scale = code_limit / jnp.full((1, 128), largest_old, F32)
    loads[3].wait()
    group_wait(yz_s, yz_peers, 3)
    totals = jnp.sum(add_all(yz_s, n_yz), axis=1, keepdims=True)
    row_mean = totals[1:2] / total_rows
    step_rms = jnp.sqrt(row_mean * totals[0:1] / (float(total_rows) * float(total_cols)))
    factor = jnp.sqrt(row_mean) / jnp.maximum(1.0, step_rms / clip_limit)
    small_out[10:11] = jnp.broadcast_to(row_mean, (1, 128))
    row_factor = row_factor * factor

    largest = jnp.zeros((ROWS, 128), F32)
    for k in range(TILES):
        cols = pl.ds(128 * k, 128)
        update = g_buf[:, cols] * row_factor * root_col[k : k + 1]
        new_master = m_buf[:, cols] - learn_rate * update
        up_buf[:, cols] = update
        nm_buf[:, cols] = new_master
        code_buf[:, cols] = jnp.clip(new_master * scale, -code_limit, code_limit).astype(jnp.bfloat16)
        largest = jnp.maximum(largest, jnp.abs(new_master))
    xz_m[c] = jnp.max(largest, axis=0, keepdims=True)
    group_start(xz_m, c, xz_peers, 4)

    top, bottom = pl.ds(0, HALF), pl.ds(HALF, HALF)
    to_right = [
        remote(code_buf.at[part], codes_out.at[d, part], ag_send.at[i], ag_recv.at[i], right)
        for i, part in enumerate((top, bottom))
    ]
    to_left = [
        remote(code_buf.at[part], codes_out.at[d, part], ag_send.at[2 + i], ag_recv.at[2 + i], left)
        for i, part in enumerate((bottom, top))
    ]
    for i in range(2):
        to_right[i].start()
        to_left[i].start()
    stores = [
        pltpu.make_async_copy(code_buf, codes_out.at[d], loc.at[6]),
        pltpu.make_async_copy(nm_buf, nm_out, loc.at[7]),
        pltpu.make_async_copy(up_buf, up_out, loc.at[8]),
    ]
    for cp in stores:
        cp.start()
    to_right[0].wait_recv()
    on_right = remote(
        codes_out.at[dp_, top], codes_out.at[dp_, top], ag_send.at[4], ag_recv.at[4], right
    )
    on_right.start()
    to_left[0].wait_recv()
    on_left = remote(
        codes_out.at[dn, bottom], codes_out.at[dn, bottom], ag_send.at[5], ag_recv.at[5], left
    )
    on_left.start()

    def max_all(buf, n):
        total = buf[0]
        for k in range(1, n):
            total = jnp.maximum(total, buf[k])
        return total

    group_wait(xz_m, xz_peers, 4)
    core_m[0] = max_all(xz_m, n_col)
    core_m_copy = remote(core_m.at[0], core_m.at[1], core_send.at[2], core_recv.at[2], mate)
    core_m_copy.start()
    core_m_copy.wait_recv()
    yz_m[q] = jnp.maximum(core_m[0], core_m[1])
    group_start(yz_m, q, yz_peers, 5)

    for cp in stores:
        cp.wait()
    for a, b in first:
        a.wait_send()
        b.wait_send()
    plain_r.wait_send()
    plain_l.wait_send()
    for m, n in merged:
        m.wait_send()
        n.wait_send()
    core_c_copy.wait_send()
    core_s_copy.wait_send()
    core_m_copy.wait_send()
    group_done(xz_r, xz_peers, 0)
    group_done(yz_c, yz_peers, 1)
    group_done(xz_t, xz_peers, 2)
    group_done(yz_s, yz_peers, 3)
    group_done(xz_m, xz_peers, 4)
    to_right[1].wait_recv()
    to_left[1].wait_recv()
    on_right.wait_recv()
    on_left.wait_recv()
    group_wait(yz_m, yz_peers, 5)
    newest = jnp.max(max_all(yz_m, n_yz), axis=1, keepdims=True)
    small_out[9:10] = jnp.broadcast_to(newest, (1, 128))
    small_out[11:16] = jnp.zeros((5, 128), F32)
    for cp in (*to_right, *to_left, on_right, on_left):
        cp.wait_send()
    group_done(yz_m, yz_peers, 5)


def finish_kernel(
    nm_in, up_in, codes_in, small, history,
    nm_out, up_out, row_out, col_out, codes_out, history_out, mean_out, sems,
):
    copies = [
        pltpu.make_async_copy(codes_in, codes_out, sems.at[0]),
        pltpu.make_async_copy(nm_in, nm_out, sems.at[1]),
        pltpu.make_async_copy(up_in, up_out, sems.at[2]),
    ]
    for cp in copies:
        cp.start()
    row_out[...] = small[8:9]
    for k in range(TILES):
        col_out[pl.ds(128 * k, 128)] = small[k]
    for i in range(15):
        history_out[i] = history[i + 1]
    history_out[15] = jnp.max(small[9:10])
    mean_out[0] = jnp.max(small[10:11])
    for cp in copies:
        cp.wait()


def body(sizes, grad, master, row_prev, col_prev, history):
    n_dp, n_row, n_col = sizes
    n_yz = n_dp * n_row // 2
    bf = jnp.bfloat16
    anywhere = pl.BlockSpec(memory_space=pl.ANY)
    vmem = pl.BlockSpec(memory_space=pltpu.VMEM)
    smem = pl.BlockSpec(memory_space=pltpu.SMEM)
    block = jax.ShapeDtypeStruct((ROWS, COLS), F32)
    codes = jax.ShapeDtypeStruct((n_dp, ROWS, COLS), bf)
    V = pltpu.VMEM
    dma = pltpu.SemaphoreType.DMA
    new_master, update, coded, small = pl.pallas_call(
        functools.partial(step_kernel, sizes),
        out_shape=[block, block, codes, jax.ShapeDtypeStruct((16, 128), F32)],
        in_specs=[anywhere, anywhere, anywhere, anywhere, smem],
        out_specs=[anywhere, anywhere, anywhere, vmem],
        scratch_shapes=[
            V((HALF, COLS), bf), V((HALF, COLS), bf),
            V((ROWS, COLS), bf), V((ROWS, COLS), bf), V((ROWS, COLS), bf),
            V((HALF, COLS), bf), V((HALF, COLS), bf), V((HALF, COLS), bf), V((HALF, COLS), bf),
            V((ROWS, COLS), F32), V((ROWS, COLS), F32), V((ROWS, COLS), F32), V((ROWS, COLS), F32),
            V((ROWS, COLS), bf), V((ROWS, 128), F32), V((1, 128), F32), V((COLS,), F32),
            V((2, 8, 128), F32), V((n_yz, 8, 128), F32),
            V((n_col, 1, 128), F32), V((n_col, 1, 128), F32),
            V((2, 2, 128), F32), V((n_yz, 2, 128), F32),
            V((n_col, 1, 128), F32), V((2, 1, 128), F32), V((n_yz, 1, 128), F32),
            dma((10,)), dma((10,)), dma((9,)), dma((3,)), dma((3,)), dma((6,)), dma((6,)), dma((6,)), dma((6,)),
        ],
        compiler_params=pltpu.CompilerParams(
            collective_id=0, has_side_effects=True, vmem_limit_bytes=16 * 1024 * 1024
        ),
        name="step",
    )(grad, master, row_prev, col_prev, history)
    new_master, update, row_new, col_new, coded, new_history, row_mean = pl.pallas_call(
        finish_kernel,
        out_shape=[
            block, block, jax.ShapeDtypeStruct((1, ROWS), F32), jax.ShapeDtypeStruct((COLS,), F32), codes,
            jax.ShapeDtypeStruct((16,), F32), jax.ShapeDtypeStruct((1,), F32),
        ],
        in_specs=[anywhere, anywhere, anywhere, vmem, smem],
        out_specs=[anywhere, anywhere, vmem, vmem, anywhere, smem, smem],
        scratch_shapes=[dma((3,))],
        name="finish",
    )(new_master, update, coded, small, history)
    return (
        new_master[None], update[None], row_new, col_new, coded, new_history, row_mean.reshape(()),
    )


def solution(mesh):
    sizes = tuple(mesh.shape[a] for a in ("dp", "row", "col"))
    placed = (P("dp", None, "row", "col"), P("dp", "row", "col"), P("dp", "row"), P("col"), P())
    return jax.shard_map(
        functools.partial(body, sizes),
        mesh=mesh,
        in_specs=placed,
        out_specs=(
            P("dp", "row", "col"),
            P("dp", "row", "col"),
            P("dp", "row"),
            P("col"),
            P(None, "row", "col"),
            P(),
            P(),
        ),
        check_vma=False,
    )
```

```python
import functools

import jax
import jax.numpy as jnp
from jax import lax
from jax.experimental import pallas as pl
from jax.experimental.pallas import tpu as pltpu
from jax.sharding import PartitionSpec as P

MESH = pl.DeviceIdType.MESH
F32 = jnp.float32

decay_rate = 0.9
epsilon = 1e-30
learn_rate = 0.01
clip_limit = 1.0
code_limit = 4.0

ROWS, COLS = 128, 1024
HALF = ROWS // 2
CHUNK = 32
TILES = COLS // 128


def whole_wait(view, sem):
    pltpu.make_async_copy(view, view, sem).wait()


def far_first(n):
    return sorted(range(n), key=lambda k: -min(k, n - k))


def step_kernel(
    sizes, grad, master, row_prev, col_prev, history,
    nm_out, up_out, codes_out, row_out, col_out, tail_out,
    merge_r, merge_l, from_l, from_r, own, next_own, prev_own, sum_r, sum_l,
    g_buf, m_buf, rowp, rm_buf, cm_buf, old,
    core_c, yz_c, xz_r, xz_t, core_s, yz_s, xz_m, core_m, yz_m,
    rs_send, rs_recv, loc, core_send, core_recv, grp_send, grp_recv, ag_send, ag_recv,
):
    n_dp, n_row, n_col = sizes
    n_zl = n_row // 2
    n_yz = n_dp * n_zl
    total_rows, total_cols = n_dp * n_row * ROWS, n_col * COLS
    d, r, c = lax.axis_index("dp"), lax.axis_index("row"), lax.axis_index("col")
    n_x = min(n_col, 4)
    n_zh = n_col // n_x
    zl, core = r // 2, r % 2
    zh, x = c // n_x, c % n_x
    q = d * n_zl + zl
    dn, dp_, do = lax.rem(d + 1, n_dp), lax.rem(d + n_dp - 1, n_dp), lax.rem(d + 2, n_dp)
    right, left = (dn, r, c), (dp_, r, c)
    mate = (d, zl * 2 + (1 - core), c)
    yz_peers = [
        (lax.rem(d + i, n_dp), lax.rem(zl + j, n_zl) * 2 + core, c)
        for i in far_first(n_dp)
        for j in far_first(n_zl)
        if i or j
    ]
    xz_peers = [
        (d, r, lax.rem(zh + i, n_zh) * n_x + lax.rem(x + j, n_x))
        for i in far_first(n_zh)
        for j in far_first(n_x)
        if i or j
    ]
    contacts = [*yz_peers, mate, *xz_peers]

    def remote(src, dst, send, recv, to):
        return pltpu.make_async_remote_copy(
            src, dst, send, recv, device_id=to, device_id_type=MESH
        )

    loads = [
        pltpu.make_async_copy(grad.at[0, d], own, loc.at[0]),
        pltpu.make_async_copy(grad.at[0, dn, pl.ds(0, HALF)], next_own, loc.at[1]),
        pltpu.make_async_copy(grad.at[0, dp_, pl.ds(HALF, HALF)], prev_own, loc.at[2]),
        pltpu.make_async_copy(master.at[0], m_buf, loc.at[3]),
        pltpu.make_async_copy(row_prev, rm_buf, loc.at[4]),
        pltpu.make_async_copy(col_prev, cm_buf, loc.at[5]),
        pltpu.make_async_copy(history, old, loc.at[6]),
    ]

    barrier = pltpu.get_barrier_semaphore()
    for p in contacts:
        pl.semaphore_signal(barrier, inc=1, device_id=p, device_id_type=MESH)
    for cp in loads:
        cp.start()
    pl.semaphore_wait(barrier, len(contacts))

    n_half = HALF // CHUNK
    sends = []
    first = []
    for i in range(n_half):
        lo, hi = pl.ds(CHUNK * i, CHUNK), pl.ds(HALF + CHUNK * i, CHUNK)
        here = pl.ds(CHUNK * i, CHUNK)
        a = remote(grad.at[0, do, lo], merge_r.at[here], rs_send.at[i], rs_recv.at[i], right)
        b = remote(grad.at[0, do, hi], merge_l.at[here], rs_send.at[2 + i], rs_recv.at[2 + i], left)
        a.start()
        b.start()
        first.append((a, b))
    plain_r = remote(
        grad.at[0, dn, pl.ds(HALF, HALF)], from_l.at[pl.ds(HALF, HALF)], rs_send.at[4], rs_recv.at[4], right
    )
    plain_l = remote(
        grad.at[0, dp_, pl.ds(0, HALF)], from_r.at[pl.ds(0, HALF)], rs_send.at[5], rs_recv.at[5], left
    )
    plain_r.start()
    plain_l.start()
    loads[1].wait()
    loads[2].wait()
    merged = []
    for i in range(n_half):
        here, hi = pl.ds(CHUNK * i, CHUNK), pl.ds(HALF + CHUNK * i, CHUNK)
        a, b = first[i]
        a.wait_recv()
        sum_r[here] = (next_own[here].astype(F32) + merge_r[here].astype(F32)).astype(jnp.bfloat16)
        m = remote(sum_r.at[here], from_l.at[here], rs_send.at[6 + i], rs_recv.at[6 + i], right)
        m.start()
        b.wait_recv()
        sum_l[here] = (prev_own[here].astype(F32) + merge_l[here].astype(F32)).astype(jnp.bfloat16)
        n = remote(sum_l.at[here], from_r.at[hi], rs_send.at[8 + i], rs_recv.at[8 + i], left)
        n.start()
        merged.append((m, n))

    loads[0].wait()
    plain_r.wait_recv()
    plain_l.wait_recv()
    col_sum = jnp.zeros((8, COLS), F32)
    for i in range(n_half):
        m, n = merged[i]
        for half, cp in ((0, m), (1, n)):
            cp.wait_recv()
            rows = pl.ds(HALF * half + CHUNK * i, CHUNK)
            g = own[rows].astype(F32) + from_l[rows].astype(F32) + from_r[rows].astype(F32)
            g_buf[rows] = g
            square = g * g + epsilon
            for j in range(CHUNK // 8):
                col_sum = col_sum + square[8 * j : 8 * j + 8]
            lanes = square[:, 0:128]
            for k in range(1, TILES):
                lanes = lanes + square[:, 128 * k : 128 * k + 128]
            rowp[rows] = lanes

    flat = jnp.sum(col_sum, axis=0, keepdims=True)
    packed = jnp.concatenate([flat[:, 128 * k : 128 * k + 128] for k in range(TILES)], axis=0)
    core_c[0] = packed
    core_c_copy = remote(core_c.at[0], core_c.at[1], core_send.at[0], core_recv.at[0], mate)
    core_c_copy.start()

    def group_start(buf, mine, peers, i):
        for p in peers:
            remote(buf.at[mine], buf.at[mine], grp_send.at[i], grp_recv.at[i], p).start()

    def group_wait(buf, peers, i):
        whole_wait(buf.at[pl.ds(0, len(peers))], grp_recv.at[i])

    def group_done(buf, peers, i):
        whole_wait(buf.at[pl.ds(0, len(peers))], grp_send.at[i])

    def add_all(buf, n):
        total = buf[0]
        for k in range(1, n):
            total = total + buf[k]
        return total

    def lanes_to_row(values):
        return jnp.sum(values.T, axis=0, keepdims=True)

    def row_to_lanes(values):
        return jnp.broadcast_to(values, (128, 128)).T

    xz_r[c] = lanes_to_row(rowp[...])
    group_start(xz_r, c, xz_peers, 0)
    core_c_copy.wait_recv()
    yz_c[q] = core_c[0] + core_c[1]
    group_start(yz_c, q, yz_peers, 1)
    loads[4].wait()
    loads[5].wait()
    group_wait(yz_c, yz_peers, 1)
    col_total = add_all(yz_c, n_yz)
    col_old = jnp.concatenate(
        [cm_buf[pl.ds(128 * k, 128)].reshape(1, 128) for k in range(TILES)], axis=0
    )
    col_new = decay_rate * col_old + (1.0 - decay_rate) * (col_total / total_rows)
    for k in range(TILES):
        col_out[pl.ds(128 * k, 128)] = col_new[k]
    inv_col = 1.0 / col_new
    root_col = 1.0 / jnp.sqrt(col_new)

    lanes = jnp.zeros((ROWS, 128), F32)
    for k in range(TILES):
        g = g_buf[:, pl.ds(128 * k, 128)]
        lanes = lanes + g * g * inv_col[k : k + 1]
    xz_t[c] = lanes_to_row(lanes)
    group_start(xz_t, c, xz_peers, 2)
    group_wait(xz_r, xz_peers, 0)
    row_total = add_all(xz_r, n_col)
    row_new = decay_rate * rm_buf[...] + (1.0 - decay_rate) * (row_total / total_cols)
    row_out[...] = row_new
    row_factor = row_to_lanes(1.0 / jnp.sqrt(row_new))
    group_wait(xz_t, xz_peers, 2)
    weighted = add_all(xz_t, n_col) / row_new

    core_s[0] = jnp.concatenate([weighted, row_new], axis=0)
    core_s_copy = remote(core_s.at[0], core_s.at[1], core_send.at[1], core_recv.at[1], mate)
    core_s_copy.start()
    core_s_copy.wait_recv()
    yz_s[q] = core_s[0] + core_s[1]
    group_start(yz_s, q, yz_peers, 3)
    loads[6].wait()
    largest_old = old[0]
    for i in range(1, 16):
        largest_old = jnp.maximum(largest_old, old[i])
    lane = lax.broadcasted_iota(jnp.int32, (1, 128), 1)
    shifted = jnp.zeros((1, 128), F32)
    for i in range(15):
        shifted = jnp.where(lane == i, old[i + 1], shifted)
    scale = code_limit / jnp.full((1, 128), largest_old, F32)
    loads[3].wait()
    group_wait(yz_s, yz_peers, 3)
    totals = jnp.sum(add_all(yz_s, n_yz), axis=1, keepdims=True)
    row_mean = totals[1:2] / total_rows
    step_rms = jnp.sqrt(row_mean * totals[0:1] / (float(total_rows) * float(total_cols)))
    factor = jnp.sqrt(row_mean) / jnp.maximum(1.0, step_rms / clip_limit)
    tail_out[1:2] = jnp.broadcast_to(row_mean, (1, 128))
    tail_out[2:8] = jnp.zeros((6, 128), F32)
    row_factor = row_factor * factor

    largest = jnp.zeros((ROWS, 128), F32)
    for k in range(TILES):
        cols = pl.ds(128 * k, 128)
        update = g_buf[:, cols] * row_factor * root_col[k : k + 1]
        new_master = m_buf[:, cols] - learn_rate * update
        up_out[:, cols] = update
        nm_out[:, cols] = new_master
        codes_out[d, :, cols] = jnp.clip(new_master * scale, -code_limit, code_limit).astype(jnp.bfloat16)
        largest = jnp.maximum(largest, jnp.abs(new_master))
    xz_m[c] = jnp.max(largest, axis=0, keepdims=True)
    group_start(xz_m, c, xz_peers, 4)

    top, bottom = pl.ds(0, HALF), pl.ds(HALF, HALF)
    to_right = [
        remote(codes_out.at[d, part], codes_out.at[d, part], ag_send.at[i], ag_recv.at[i], right)
        for i, part in enumerate((top, bottom))
    ]
    to_left = [
        remote(codes_out.at[d, part], codes_out.at[d, part], ag_send.at[2 + i], ag_recv.at[2 + i], left)
        for i, part in enumerate((bottom, top))
    ]
    for i in range(2):
        to_right[i].start()
        to_left[i].start()
    to_right[0].wait_recv()
    on_right = remote(
        codes_out.at[dp_, top], codes_out.at[dp_, top], ag_send.at[4], ag_recv.at[4], right
    )
    on_right.start()
    to_left[0].wait_recv()
    on_left = remote(
        codes_out.at[dn, bottom], codes_out.at[dn, bottom], ag_send.at[5], ag_recv.at[5], left
    )
    on_left.start()

    def max_all(buf, n):
        total = buf[0]
        for k in range(1, n):
            total = jnp.maximum(total, buf[k])
        return total

    group_wait(xz_m, xz_peers, 4)
    core_m[0] = max_all(xz_m, n_col)
    core_m_copy = remote(core_m.at[0], core_m.at[1], core_send.at[2], core_recv.at[2], mate)
    core_m_copy.start()
    core_m_copy.wait_recv()
    yz_m[q] = jnp.maximum(core_m[0], core_m[1])
    group_start(yz_m, q, yz_peers, 5)

    for a, b in first:
        a.wait_send()
        b.wait_send()
    plain_r.wait_send()
    plain_l.wait_send()
    for m, n in merged:
        m.wait_send()
        n.wait_send()
    core_c_copy.wait_send()
    core_s_copy.wait_send()
    core_m_copy.wait_send()
    group_done(xz_r, xz_peers, 0)
    group_done(yz_c, yz_peers, 1)
    group_done(xz_t, xz_peers, 2)
    group_done(yz_s, yz_peers, 3)
    group_done(xz_m, xz_peers, 4)
    to_right[1].wait_recv()
    to_left[1].wait_recv()
    on_right.wait_recv()
    on_left.wait_recv()
    group_wait(yz_m, yz_peers, 5)
    newest = jnp.max(max_all(yz_m, n_yz), axis=1, keepdims=True)
    tail_out[0:1] = jnp.where(lane == 15, newest, shifted)
    for cp in (*to_right, *to_left, on_right, on_left):
        cp.wait_send()
    group_done(yz_m, yz_peers, 5)


def finish_kernel(
    nm_in, up_in, codes_in, row_in, col_in, tail,
    nm_out, up_out, row_out, col_out, codes_out, history_out, mean_out, last, mean, sems,
):
    copies = [
        pltpu.make_async_copy(a, b, sems.at[i])
        for i, (a, b) in enumerate(
            (
                (codes_in, codes_out),
                (nm_in, nm_out),
                (up_in, up_out),
                (row_in, row_out),
                (col_in, col_out),
                (last, history_out),
                (mean, mean_out),
            )
        )
    ]
    for cp in copies[:5]:
        cp.start()
    last[...] = tail[0, 0:16]
    mean[...] = tail[1, 0:1]
    for cp in copies[5:]:
        cp.start()
    for cp in copies:
        cp.wait()


def body(sizes, grad, master, row_prev, col_prev, history):
    n_dp, n_row, n_col = sizes
    n_yz = n_dp * n_row // 2
    bf = jnp.bfloat16
    anywhere = pl.BlockSpec(memory_space=pl.ANY)
    vmem = pl.BlockSpec(memory_space=pltpu.VMEM)
    hbm = pl.BlockSpec(memory_space=pltpu.HBM)
    block = jax.ShapeDtypeStruct((ROWS, COLS), F32)
    codes = jax.ShapeDtypeStruct((n_dp, ROWS, COLS), bf)
    V = pltpu.VMEM
    dma = pltpu.SemaphoreType.DMA
    row_like, col_like = jax.ShapeDtypeStruct((1, ROWS), F32), jax.ShapeDtypeStruct((COLS,), F32)
    given = [pltpu.with_memory_space_constraint(a, pltpu.HBM) for a in (grad, master, row_prev, col_prev, history)]
    new_master, update, coded, row_new, col_new, tail = pl.pallas_call(
        functools.partial(step_kernel, sizes),
        out_shape=[block, block, codes, row_like, col_like, jax.ShapeDtypeStruct((8, 128), F32)],
        in_specs=[hbm] * 5,
        out_specs=[vmem] * 6,
        scratch_shapes=[
            V((HALF, COLS), bf), V((HALF, COLS), bf),
            V((ROWS, COLS), bf), V((ROWS, COLS), bf), V((ROWS, COLS), bf),
            V((HALF, COLS), bf), V((HALF, COLS), bf), V((HALF, COLS), bf), V((HALF, COLS), bf),
            V((ROWS, COLS), F32), V((ROWS, COLS), F32), V((ROWS, 128), F32), V((1, 128), F32), V((COLS,), F32), pltpu.SMEM((16,), F32),
            V((2, 8, 128), F32), V((n_yz, 8, 128), F32),
            V((n_col, 1, 128), F32), V((n_col, 1, 128), F32),
            V((2, 2, 128), F32), V((n_yz, 2, 128), F32),
            V((n_col, 1, 128), F32), V((2, 1, 128), F32), V((n_yz, 1, 128), F32),
            dma((10,)), dma((10,)), dma((8,)), dma((3,)), dma((3,)), dma((6,)), dma((6,)), dma((6,)), dma((6,)),
        ],
        compiler_params=pltpu.CompilerParams(
            collective_id=0, has_side_effects=True, vmem_limit_bytes=16 * 1024 * 1024
        ),
        name="step",
    )(*given)
    new_master, update, row_new, col_new, coded, new_history, row_mean = pl.pallas_call(
        finish_kernel,
        out_shape=[
            block, block, row_like, col_like, codes,
            jax.ShapeDtypeStruct((16,), F32), jax.ShapeDtypeStruct((1,), F32),
        ],
        in_specs=[anywhere] * 5 + [vmem],
        out_specs=[hbm] * 7,
        scratch_shapes=[V((16,), F32), V((1,), F32), dma((7,))],
        compiler_params=pltpu.CompilerParams(vmem_limit_bytes=1024 * 1024),
        name="finish",
    )(new_master, update, coded, row_new, col_new, tail)
    return (
        new_master[None], update[None], row_new, col_new, coded, new_history, row_mean.reshape(()),
    )


def solution(mesh):
    sizes = tuple(mesh.shape[a] for a in ("dp", "row", "col"))
    placed = (P("dp", None, "row", "col"), P("dp", "row", "col"), P("dp", "row"), P("col"), P())
    return jax.shard_map(
        functools.partial(body, sizes),
        mesh=mesh,
        in_specs=placed,
        out_specs=(
            P("dp", "row", "col"),
            P("dp", "row", "col"),
            P("dp", "row"),
            P("col"),
            P(None, "row", "col"),
            P(),
            P(),
        ),
        check_vma=False,
    )
```

```python
import functools

import jax
import jax.numpy as jnp
from jax import lax
from jax.experimental import pallas as pl
from jax.experimental.pallas import tpu as pltpu
from jax.sharding import PartitionSpec as P

MESH = pl.DeviceIdType.MESH
F32 = jnp.float32

decay_rate = 0.9
epsilon = 1e-30
learn_rate = 0.01
clip_limit = 1.0
code_limit = 4.0

ROWS, COLS = 128, 1024
HALF = ROWS // 2
CHUNK = 32
TILES = COLS // 128


def whole_wait(view, sem):
    pltpu.make_async_copy(view, view, sem).wait()


def far_first(n):
    return sorted(range(n), key=lambda k: -min(k, n - k))


def step_kernel(
    sizes, grad, master, row_prev, col_prev, history,
    nm_out, up_out, codes_out, row_out, col_out, tail_out,
    merge_r, merge_l, from_l, from_r, own, next_own, prev_own, sum_r, sum_l,
    g_buf, m_buf, rowp, rm_buf, cm_buf, old,
    core_c, yz_c, xz_r, xz_t, core_s, yz_s, xz_m, core_m, yz_m,
    rs_send, rs_recv, loc, core_send, core_recv, grp_send, grp_recv, ag_send, ag_recv, greet,
):
    n_dp, n_row, n_col = sizes
    n_zl = n_row // 2
    n_yz = n_dp * n_zl
    total_rows, total_cols = n_dp * n_row * ROWS, n_col * COLS
    d, r, c = lax.axis_index("dp"), lax.axis_index("row"), lax.axis_index("col")
    n_x = min(n_col, 4)
    n_zh = n_col // n_x
    zl, core = r // 2, r % 2
    zh, x = c // n_x, c % n_x
    q = d * n_zl + zl
    dn, dp_, do = lax.rem(d + 1, n_dp), lax.rem(d + n_dp - 1, n_dp), lax.rem(d + 2, n_dp)
    right, left = (dn, r, c), (dp_, r, c)
    mate = (d, zl * 2 + (1 - core), c)
    yz_peers = [
        (lax.rem(d + i, n_dp), lax.rem(zl + j, n_zl) * 2 + core, c)
        for i in far_first(n_dp)
        for j in far_first(n_zl)
        if i or j
    ]
    xz_peers = [
        (d, r, lax.rem(zh + i, n_zh) * n_x + lax.rem(x + j, n_x))
        for i in far_first(n_zh)
        for j in far_first(n_x)
        if i or j
    ]
    z_near = [
        (d, r, lax.rem(zh + i, n_zh) * n_x + x) for i in sorted({1 % n_zh, n_zh - 1} - {0})
    ]
    near = [(lax.rem(d + i, n_dp), r, c) for i in far_first(n_dp) if i]
    near += [(d, lax.rem(zl + j, n_zl) * 2 + core, c) for j in far_first(n_zl) if j]
    near += [(d, r, zh * n_x + lax.rem(x + j, n_x)) for j in far_first(n_x) if j]
    near += z_near
    contacts = [*near, mate]

    def remote(src, dst, send, recv, to):
        return pltpu.make_async_remote_copy(
            src, dst, send, recv, device_id=to, device_id_type=MESH
        )

    loads = [
        pltpu.make_async_copy(grad.at[0, d], own, loc.at[0]),
        pltpu.make_async_copy(grad.at[0, dn, pl.ds(0, HALF)], next_own, loc.at[1]),
        pltpu.make_async_copy(grad.at[0, dp_, pl.ds(HALF, HALF)], prev_own, loc.at[2]),
        pltpu.make_async_copy(master.at[0], m_buf, loc.at[3]),
        pltpu.make_async_copy(row_prev, rm_buf, loc.at[4]),
        pltpu.make_async_copy(col_prev, cm_buf, loc.at[5]),
        pltpu.make_async_copy(history, old, loc.at[6]),
    ]

    barrier = pltpu.get_barrier_semaphore()
    for p in contacts:
        pl.semaphore_signal(barrier, inc=1, device_id=p, device_id_type=MESH)
    for cp in loads:
        cp.start()
    pl.semaphore_wait(barrier, len(contacts))

    n_half = HALF // CHUNK
    sends = []
    first = []
    for i in range(n_half):
        lo, hi = pl.ds(CHUNK * i, CHUNK), pl.ds(HALF + CHUNK * i, CHUNK)
        here = pl.ds(CHUNK * i, CHUNK)
        a = remote(grad.at[0, do, lo], merge_r.at[here], rs_send.at[i], rs_recv.at[i], right)
        b = remote(grad.at[0, do, hi], merge_l.at[here], rs_send.at[2 + i], rs_recv.at[2 + i], left)
        a.start()
        b.start()
        first.append((a, b))
    plain_r = remote(
        grad.at[0, dn, pl.ds(HALF, HALF)], from_l.at[pl.ds(HALF, HALF)], rs_send.at[4], rs_recv.at[4], right
    )
    plain_l = remote(
        grad.at[0, dp_, pl.ds(0, HALF)], from_r.at[pl.ds(0, HALF)], rs_send.at[5], rs_recv.at[5], left
    )
    plain_r.start()
    plain_l.start()
    for p in near:
        pl.semaphore_signal(greet.at[0], inc=1, device_id=p, device_id_type=MESH)
    loads[1].wait()
    loads[2].wait()
    merged = []
    for i in range(n_half):
        here, hi = pl.ds(CHUNK * i, CHUNK), pl.ds(HALF + CHUNK * i, CHUNK)
        a, b = first[i]
        a.wait_recv()
        sum_r[here] = (next_own[here].astype(F32) + merge_r[here].astype(F32)).astype(jnp.bfloat16)
        m = remote(sum_r.at[here], from_l.at[here], rs_send.at[6 + i], rs_recv.at[6 + i], right)
        m.start()
        b.wait_recv()
        sum_l[here] = (prev_own[here].astype(F32) + merge_l[here].astype(F32)).astype(jnp.bfloat16)
        n = remote(sum_l.at[here], from_r.at[hi], rs_send.at[8 + i], rs_recv.at[8 + i], left)
        n.start()
        merged.append((m, n))

    pl.semaphore_wait(greet.at[0], len(near))
    for p in z_near:
        pl.semaphore_signal(greet.at[1], inc=1, device_id=p, device_id_type=MESH)
    loads[0].wait()
    plain_r.wait_recv()
    plain_l.wait_recv()
    col_sum = jnp.zeros((8, COLS), F32)
    for i in range(n_half):
        m, n = merged[i]
        for half, cp in ((0, m), (1, n)):
            cp.wait_recv()
            rows = pl.ds(HALF * half + CHUNK * i, CHUNK)
            g = own[rows].astype(F32) + from_l[rows].astype(F32) + from_r[rows].astype(F32)
            g_buf[rows] = g
            square = g * g + epsilon
            for j in range(CHUNK // 8):
                col_sum = col_sum + square[8 * j : 8 * j + 8]
            lanes = square[:, 0:128]
            for k in range(1, TILES):
                lanes = lanes + square[:, 128 * k : 128 * k + 128]
            rowp[rows] = lanes

    flat = jnp.sum(col_sum, axis=0, keepdims=True)
    packed = jnp.concatenate([flat[:, 128 * k : 128 * k + 128] for k in range(TILES)], axis=0)
    core_c[0] = packed
    core_c_copy = remote(core_c.at[0], core_c.at[1], core_send.at[0], core_recv.at[0], mate)
    core_c_copy.start()

    def group_start(buf, mine, peers, i):
        for p in peers:
            remote(buf.at[mine], buf.at[mine], grp_send.at[i], grp_recv.at[i], p).start()

    def group_wait(buf, peers, i):
        whole_wait(buf.at[pl.ds(0, len(peers))], grp_recv.at[i])

    def group_done(buf, peers, i):
        whole_wait(buf.at[pl.ds(0, len(peers))], grp_send.at[i])

    def add_all(buf, n):
        total = buf[0]
        for k in range(1, n):
            total = total + buf[k]
        return total

    def lanes_to_row(values):
        return jnp.sum(values.T, axis=0, keepdims=True)

    def row_to_lanes(values):
        return jnp.broadcast_to(values, (128, 128)).T

    xz_r[c] = lanes_to_row(rowp[...])
    if z_near:
        pl.semaphore_wait(greet.at[1], len(z_near))
    group_start(xz_r, c, xz_peers, 0)
    core_c_copy.wait_recv()
    yz_c[q] = core_c[0] + core_c[1]
    group_start(yz_c, q, yz_peers, 1)
    loads[4].wait()
    loads[5].wait()
    group_wait(yz_c, yz_peers, 1)
    col_total = add_all(yz_c, n_yz)
    col_old = jnp.concatenate(
        [cm_buf[pl.ds(128 * k, 128)].reshape(1, 128) for k in range(TILES)], axis=0
    )
    col_new = decay_rate * col_old + (1.0 - decay_rate) * (col_total / total_rows)
    for k in range(TILES):
        col_out[pl.ds(128 * k, 128)] = col_new[k]
    inv_col = 1.0 / col_new
    root_col = 1.0 / jnp.sqrt(col_new)

    lanes = jnp.zeros((ROWS, 128), F32)
    for k in range(TILES):
        g = g_buf[:, pl.ds(128 * k, 128)]
        lanes = lanes + g * g * inv_col[k : k + 1]
    xz_t[c] = lanes_to_row(lanes)
    group_start(xz_t, c, xz_peers, 2)
    group_wait(xz_r, xz_peers, 0)
    row_total = add_all(xz_r, n_col)
    row_new = decay_rate * rm_buf[...] + (1.0 - decay_rate) * (row_total / total_cols)
    row_out[...] = row_new
    row_factor = row_to_lanes(1.0 / jnp.sqrt(row_new))
    group_wait(xz_t, xz_peers, 2)
    weighted = add_all(xz_t, n_col) / row_new

    core_s[0] = jnp.concatenate([weighted, row_new], axis=0)
    core_s_copy = remote(core_s.at[0], core_s.at[1], core_send.at[1], core_recv.at[1], mate)
    core_s_copy.start()
    core_s_copy.wait_recv()
    yz_s[q] = core_s[0] + core_s[1]
    group_start(yz_s, q, yz_peers, 3)
    loads[6].wait()
    largest_old = old[0]
    for i in range(1, 16):
        largest_old = jnp.maximum(largest_old, old[i])
    lane = lax.broadcasted_iota(jnp.int32, (1, 128), 1)
    shifted = jnp.zeros((1, 128), F32)
    for i in range(15):
        shifted = jnp.where(lane == i, old[i + 1], shifted)
    scale = code_limit / jnp.full((1, 128), largest_old, F32)
    loads[3].wait()
    group_wait(yz_s, yz_peers, 3)
    totals = jnp.sum(add_all(yz_s, n_yz), axis=1, keepdims=True)
    row_mean = totals[1:2] / total_rows
    step_rms = jnp.sqrt(row_mean * totals[0:1] / (float(total_rows) * float(total_cols)))
    factor = jnp.sqrt(row_mean) / jnp.maximum(1.0, step_rms / clip_limit)
    tail_out[1:2] = jnp.broadcast_to(row_mean, (1, 128))
    tail_out[2:8] = jnp.zeros((6, 128), F32)
    row_factor = row_factor * factor

    largest = jnp.zeros((ROWS, 128), F32)
    for k in range(TILES):
        cols = pl.ds(128 * k, 128)
        update = g_buf[:, cols] * row_factor * root_col[k : k + 1]
        new_master = m_buf[:, cols] - learn_rate * update
        up_out[:, cols] = update
        nm_out[:, cols] = new_master
        codes_out[d, :, cols] = jnp.clip(new_master * scale, -code_limit, code_limit).astype(jnp.bfloat16)
        largest = jnp.maximum(largest, jnp.abs(new_master))
    xz_m[c] = jnp.max(largest, axis=0, keepdims=True)
    group_start(xz_m, c, xz_peers, 4)

    top, bottom = pl.ds(0, HALF), pl.ds(HALF, HALF)
    to_right = [
        remote(codes_out.at[d, part], codes_out.at[d, part], ag_send.at[i], ag_recv.at[i], right)
        for i, part in enumerate((top, bottom))
    ]
    to_left = [
        remote(codes_out.at[d, part], codes_out.at[d, part], ag_send.at[2 + i], ag_recv.at[2 + i], left)
        for i, part in enumerate((bottom, top))
    ]
    for i in range(2):
        to_right[i].start()
        to_left[i].start()
    to_right[0].wait_recv()
    on_right = remote(
        codes_out.at[dp_, top], codes_out.at[dp_, top], ag_send.at[4], ag_recv.at[4], right
    )
    on_right.start()
    to_left[0].wait_recv()
    on_left = remote(
        codes_out.at[dn, bottom], codes_out.at[dn, bottom], ag_send.at[5], ag_recv.at[5], left
    )
    on_left.start()

    def max_all(buf, n):
        total = buf[0]
        for k in range(1, n):
            total = jnp.maximum(total, buf[k])
        return total

    group_wait(xz_m, xz_peers, 4)
    core_m[0] = max_all(xz_m, n_col)
    core_m_copy = remote(core_m.at[0], core_m.at[1], core_send.at[2], core_recv.at[2], mate)
    core_m_copy.start()
    core_m_copy.wait_recv()
    yz_m[q] = jnp.maximum(core_m[0], core_m[1])
    group_start(yz_m, q, yz_peers, 5)

    for a, b in first:
        a.wait_send()
        b.wait_send()
    plain_r.wait_send()
    plain_l.wait_send()
    for m, n in merged:
        m.wait_send()
        n.wait_send()
    core_c_copy.wait_send()
    core_s_copy.wait_send()
    core_m_copy.wait_send()
    group_done(xz_r, xz_peers, 0)
    group_done(yz_c, yz_peers, 1)
    group_done(xz_t, xz_peers, 2)
    group_done(yz_s, yz_peers, 3)
    group_done(xz_m, xz_peers, 4)
    to_right[1].wait_recv()
    to_left[1].wait_recv()
    on_right.wait_recv()
    on_left.wait_recv()
    group_wait(yz_m, yz_peers, 5)
    newest = jnp.max(max_all(yz_m, n_yz), axis=1, keepdims=True)
    tail_out[0:1] = jnp.where(lane == 15, newest, shifted)
    for cp in (*to_right, *to_left, on_right, on_left):
        cp.wait_send()
    group_done(yz_m, yz_peers, 5)


def finish_kernel(
    nm_in, up_in, codes_in, row_in, col_in, tail,
    nm_out, up_out, row_out, col_out, codes_out, history_out, mean_out, last, mean, sems,
):
    copies = [
        pltpu.make_async_copy(a, b, sems.at[i])
        for i, (a, b) in enumerate(
            (
                (codes_in, codes_out),
                (nm_in, nm_out),
                (up_in, up_out),
                (row_in, row_out),
                (col_in, col_out),
                (last, history_out),
                (mean, mean_out),
            )
        )
    ]
    for cp in copies[:5]:
        cp.start()
    last[...] = tail[0, 0:16]
    mean[...] = tail[1, 0:1]
    for cp in copies[5:]:
        cp.start()
    for cp in copies:
        cp.wait()


def body(sizes, grad, master, row_prev, col_prev, history):
    n_dp, n_row, n_col = sizes
    n_yz = n_dp * n_row // 2
    bf = jnp.bfloat16
    anywhere = pl.BlockSpec(memory_space=pl.ANY)
    vmem = pl.BlockSpec(memory_space=pltpu.VMEM)
    hbm = pl.BlockSpec(memory_space=pltpu.HBM)
    block = jax.ShapeDtypeStruct((ROWS, COLS), F32)
    codes = jax.ShapeDtypeStruct((n_dp, ROWS, COLS), bf)
    V = pltpu.VMEM
    dma = pltpu.SemaphoreType.DMA
    row_like, col_like = jax.ShapeDtypeStruct((1, ROWS), F32), jax.ShapeDtypeStruct((COLS,), F32)
    given = [pltpu.with_memory_space_constraint(a, pltpu.HBM) for a in (grad, master, row_prev, col_prev, history)]
    new_master, update, coded, row_new, col_new, tail = pl.pallas_call(
        functools.partial(step_kernel, sizes),
        out_shape=[block, block, codes, row_like, col_like, jax.ShapeDtypeStruct((8, 128), F32)],
        in_specs=[hbm] * 5,
        out_specs=[vmem] * 6,
        scratch_shapes=[
            V((HALF, COLS), bf), V((HALF, COLS), bf),
            V((ROWS, COLS), bf), V((ROWS, COLS), bf), V((ROWS, COLS), bf),
            V((HALF, COLS), bf), V((HALF, COLS), bf), V((HALF, COLS), bf), V((HALF, COLS), bf),
            V((ROWS, COLS), F32), V((ROWS, COLS), F32), V((ROWS, 128), F32), V((1, 128), F32), V((COLS,), F32), pltpu.SMEM((16,), F32),
            V((2, 8, 128), F32), V((n_yz, 8, 128), F32),
            V((n_col, 1, 128), F32), V((n_col, 1, 128), F32),
            V((2, 2, 128), F32), V((n_yz, 2, 128), F32),
            V((n_col, 1, 128), F32), V((2, 1, 128), F32), V((n_yz, 1, 128), F32),
            dma((10,)), dma((10,)), dma((8,)), dma((3,)), dma((3,)), dma((6,)), dma((6,)), dma((6,)), dma((6,)),
            pltpu.SemaphoreType.REGULAR((2,)),
        ],
        compiler_params=pltpu.CompilerParams(
            collective_id=0, has_side_effects=True, vmem_limit_bytes=16 * 1024 * 1024
        ),
        name="step",
    )(*given)
    new_master, update, row_new, col_new, coded, new_history, row_mean = pl.pallas_call(
        finish_kernel,
        out_shape=[
            block, block, row_like, col_like, codes,
            jax.ShapeDtypeStruct((16,), F32), jax.ShapeDtypeStruct((1,), F32),
        ],
        in_specs=[anywhere] * 5 + [vmem],
        out_specs=[hbm] * 7,
        scratch_shapes=[V((16,), F32), V((1,), F32), dma((7,))],
        compiler_params=pltpu.CompilerParams(vmem_limit_bytes=1024 * 1024),
        name="finish",
    )(new_master, update, coded, row_new, col_new, tail)
    return (
        new_master[None], update[None], row_new, col_new, coded, new_history, row_mean.reshape(()),
    )


def solution(mesh):
    sizes = tuple(mesh.shape[a] for a in ("dp", "row", "col"))
    placed = (P("dp", None, "row", "col"), P("dp", "row", "col"), P("dp", "row"), P("col"), P())
    return jax.shard_map(
        functools.partial(body, sizes),
        mesh=mesh,
        in_specs=placed,
        out_specs=(
            P("dp", "row", "col"),
            P("dp", "row", "col"),
            P("dp", "row"),
            P("col"),
            P(None, "row", "col"),
            P(),
            P(),
        ),
        check_vma=False,
    )
```

```python
import functools

import jax
import jax.numpy as jnp
from jax import lax
from jax.experimental import pallas as pl
from jax.experimental.pallas import tpu as pltpu
from jax.sharding import PartitionSpec as P

MESH = pl.DeviceIdType.MESH
F32 = jnp.float32

decay_rate = 0.9
epsilon = 1e-30
learn_rate = 0.01
clip_limit = 1.0
code_limit = 4.0

ROWS, COLS = 128, 1024
HALF = ROWS // 2
CHUNK = 32
TILES = COLS // 128


def whole_wait(view, sem):
    pltpu.make_async_copy(view, view, sem).wait()


def far_first(n):
    return sorted(range(n), key=lambda k: -min(k, n - k))


def step_kernel(
    sizes, grad, master, row_prev, col_prev, history,
    nm_out, up_out, codes_out, row_out, col_out, tail_out,
    merge_r, merge_l, from_l, from_r, own, next_own, prev_own, sum_r, sum_l,
    g_buf, m_buf, rowp, rm_buf, cm_buf, old,
    core_c, yz_c, xz_r, xz_t, core_s, yz_s, z_m, core_m, xy_m,
    rs_send, rs_recv, loc, core_send, core_recv, grp_send, grp_recv, ag_send, ag_recv, greet,
):
    n_dp, n_row, n_col = sizes
    n_zl = n_row // 2
    n_yz = n_dp * n_zl
    total_rows, total_cols = n_dp * n_row * ROWS, n_col * COLS
    d, r, c = lax.axis_index("dp"), lax.axis_index("row"), lax.axis_index("col")
    n_x = min(n_col, 4)
    n_zh = n_col // n_x
    zl, core = r // 2, r % 2
    zh, x = c // n_x, c % n_x
    q = d * n_zl + zl
    dn, dp_, do = lax.rem(d + 1, n_dp), lax.rem(d + n_dp - 1, n_dp), lax.rem(d + 2, n_dp)
    right, left = (dn, r, c), (dp_, r, c)
    mate = (d, zl * 2 + (1 - core), c)
    yz_peers = [
        (lax.rem(d + i, n_dp), lax.rem(zl + j, n_zl) * 2 + core, c)
        for i in far_first(n_dp)
        for j in far_first(n_zl)
        if i or j
    ]
    xz_peers = [
        (d, r, lax.rem(zh + i, n_zh) * n_x + lax.rem(x + j, n_x))
        for i in far_first(n_zh)
        for j in far_first(n_x)
        if i or j
    ]
    z_near = [
        (d, r, lax.rem(zh + i, n_zh) * n_x + x) for i in sorted({1 % n_zh, n_zh - 1} - {0})
    ]
    near = [(lax.rem(d + i, n_dp), r, c) for i in far_first(n_dp) if i]
    near += [(d, lax.rem(zl + j, n_zl) * 2 + core, c) for j in far_first(n_zl) if j]
    near += [(d, r, zh * n_x + lax.rem(x + j, n_x)) for j in far_first(n_x) if j]
    near += z_near
    contacts = [*near, mate]
    z_peers = [
        (d, lax.rem(zl + j, n_zl) * 2 + core, lax.rem(zh + i, n_zh) * n_x + x)
        for i in far_first(n_zh)
        for j in far_first(n_zl)
        if i or j
    ]
    xy_peers = [
        (lax.rem(d + i, n_dp), r, zh * n_x + lax.rem(x + j, n_x))
        for i in far_first(n_dp)
        for j in far_first(n_x)
        if i or j
    ]
    z_mine, xy_mine = zh * n_zl + zl, d * n_x + x

    def remote(src, dst, send, recv, to):
        return pltpu.make_async_remote_copy(
            src, dst, send, recv, device_id=to, device_id_type=MESH
        )

    loads = [
        pltpu.make_async_copy(grad.at[0, d], own, loc.at[0]),
        pltpu.make_async_copy(grad.at[0, dn, pl.ds(0, HALF)], next_own, loc.at[1]),
        pltpu.make_async_copy(grad.at[0, dp_, pl.ds(HALF, HALF)], prev_own, loc.at[2]),
        pltpu.make_async_copy(master.at[0], m_buf, loc.at[3]),
        pltpu.make_async_copy(row_prev, rm_buf, loc.at[4]),
        pltpu.make_async_copy(col_prev, cm_buf, loc.at[5]),
        pltpu.make_async_copy(history, old, loc.at[6]),
    ]

    barrier = pltpu.get_barrier_semaphore()
    for p in contacts:
        pl.semaphore_signal(barrier, inc=1, device_id=p, device_id_type=MESH)
    for cp in loads:
        cp.start()
    pl.semaphore_wait(barrier, len(contacts))

    n_half = HALF // CHUNK
    sends = []
    first = []
    for i in range(n_half):
        lo, hi = pl.ds(CHUNK * i, CHUNK), pl.ds(HALF + CHUNK * i, CHUNK)
        here = pl.ds(CHUNK * i, CHUNK)
        a = remote(grad.at[0, do, lo], merge_r.at[here], rs_send.at[i], rs_recv.at[i], right)
        b = remote(grad.at[0, do, hi], merge_l.at[here], rs_send.at[2 + i], rs_recv.at[2 + i], left)
        a.start()
        b.start()
        first.append((a, b))
    plain_r = remote(
        grad.at[0, dn, pl.ds(HALF, HALF)], from_l.at[pl.ds(HALF, HALF)], rs_send.at[4], rs_recv.at[4], right
    )
    plain_l = remote(
        grad.at[0, dp_, pl.ds(0, HALF)], from_r.at[pl.ds(0, HALF)], rs_send.at[5], rs_recv.at[5], left
    )
    plain_r.start()
    plain_l.start()
    for p in near:
        pl.semaphore_signal(greet.at[0], inc=1, device_id=p, device_id_type=MESH)
    loads[1].wait()
    loads[2].wait()
    merged = []
    for i in range(n_half):
        here, hi = pl.ds(CHUNK * i, CHUNK), pl.ds(HALF + CHUNK * i, CHUNK)
        a, b = first[i]
        a.wait_recv()
        sum_r[here] = (next_own[here].astype(F32) + merge_r[here].astype(F32)).astype(jnp.bfloat16)
        m = remote(sum_r.at[here], from_l.at[here], rs_send.at[6 + i], rs_recv.at[6 + i], right)
        m.start()
        b.wait_recv()
        sum_l[here] = (prev_own[here].astype(F32) + merge_l[here].astype(F32)).astype(jnp.bfloat16)
        n = remote(sum_l.at[here], from_r.at[hi], rs_send.at[8 + i], rs_recv.at[8 + i], left)
        n.start()
        merged.append((m, n))

    pl.semaphore_wait(greet.at[0], len(near))
    for p in z_near:
        pl.semaphore_signal(greet.at[1], inc=1, device_id=p, device_id_type=MESH)
    loads[0].wait()
    plain_r.wait_recv()
    plain_l.wait_recv()
    col_sum = jnp.zeros((8, COLS), F32)
    for i in range(n_half):
        m, n = merged[i]
        for half, cp in ((0, m), (1, n)):
            cp.wait_recv()
            rows = pl.ds(HALF * half + CHUNK * i, CHUNK)
            g = own[rows].astype(F32) + from_l[rows].astype(F32) + from_r[rows].astype(F32)
            g_buf[rows] = g
            square = g * g + epsilon
            for j in range(CHUNK // 8):
                col_sum = col_sum + square[8 * j : 8 * j + 8]
            lanes = square[:, 0:128]
            for k in range(1, TILES):
                lanes = lanes + square[:, 128 * k : 128 * k + 128]
            rowp[rows] = lanes

    flat = jnp.sum(col_sum, axis=0, keepdims=True)
    packed = jnp.concatenate([flat[:, 128 * k : 128 * k + 128] for k in range(TILES)], axis=0)
    core_c[0] = packed
    core_c_copy = remote(core_c.at[0], core_c.at[1], core_send.at[0], core_recv.at[0], mate)
    core_c_copy.start()

    def group_start(buf, mine, peers, i):
        for p in peers:
            remote(buf.at[mine], buf.at[mine], grp_send.at[i], grp_recv.at[i], p).start()

    def group_wait(buf, peers, i):
        whole_wait(buf.at[pl.ds(0, len(peers))], grp_recv.at[i])

    def group_done(buf, peers, i):
        whole_wait(buf.at[pl.ds(0, len(peers))], grp_send.at[i])

    def add_all(buf, n):
        total = buf[0]
        for k in range(1, n):
            total = total + buf[k]
        return total

    def lanes_to_row(values):
        return jnp.sum(values.T, axis=0, keepdims=True)

    def row_to_lanes(values):
        return jnp.broadcast_to(values, (128, 128)).T

    xz_r[c] = lanes_to_row(rowp[...])
    if z_near:
        pl.semaphore_wait(greet.at[1], len(z_near))
    group_start(xz_r, c, xz_peers, 0)
    core_c_copy.wait_recv()
    yz_c[q] = core_c[0] + core_c[1]
    group_start(yz_c, q, yz_peers, 1)
    loads[4].wait()
    loads[5].wait()
    group_wait(yz_c, yz_peers, 1)
    col_total = add_all(yz_c, n_yz)
    col_old = jnp.concatenate(
        [cm_buf[pl.ds(128 * k, 128)].reshape(1, 128) for k in range(TILES)], axis=0
    )
    col_new = decay_rate * col_old + (1.0 - decay_rate) * (col_total / total_rows)
    for k in range(TILES):
        col_out[pl.ds(128 * k, 128)] = col_new[k]
    inv_col = 1.0 / col_new
    root_col = 1.0 / jnp.sqrt(col_new)

    lanes = jnp.zeros((ROWS, 128), F32)
    for k in range(TILES):
        g = g_buf[:, pl.ds(128 * k, 128)]
        lanes = lanes + g * g * inv_col[k : k + 1]
    xz_t[c] = lanes_to_row(lanes)
    group_start(xz_t, c, xz_peers, 2)
    group_wait(xz_r, xz_peers, 0)
    row_total = add_all(xz_r, n_col)
    row_new = decay_rate * rm_buf[...] + (1.0 - decay_rate) * (row_total / total_cols)
    row_out[...] = row_new
    row_factor = row_to_lanes(1.0 / jnp.sqrt(row_new))
    group_wait(xz_t, xz_peers, 2)
    weighted = add_all(xz_t, n_col) / row_new

    core_s[0] = jnp.concatenate([weighted, row_new], axis=0)
    core_s_copy = remote(core_s.at[0], core_s.at[1], core_send.at[1], core_recv.at[1], mate)
    core_s_copy.start()
    core_s_copy.wait_recv()
    yz_s[q] = core_s[0] + core_s[1]
    group_start(yz_s, q, yz_peers, 3)
    loads[6].wait()
    largest_old = old[0]
    for i in range(1, 16):
        largest_old = jnp.maximum(largest_old, old[i])
    lane = lax.broadcasted_iota(jnp.int32, (1, 128), 1)
    shifted = jnp.zeros((1, 128), F32)
    for i in range(15):
        shifted = jnp.where(lane == i, old[i + 1], shifted)
    scale = code_limit / jnp.full((1, 128), largest_old, F32)
    loads[3].wait()
    group_wait(yz_s, yz_peers, 3)
    totals = jnp.sum(add_all(yz_s, n_yz), axis=1, keepdims=True)
    row_mean = totals[1:2] / total_rows
    step_rms = jnp.sqrt(row_mean * totals[0:1] / (float(total_rows) * float(total_cols)))
    factor = jnp.sqrt(row_mean) / jnp.maximum(1.0, step_rms / clip_limit)
    tail_out[1:2] = jnp.broadcast_to(row_mean, (1, 128))
    tail_out[2:8] = jnp.zeros((6, 128), F32)
    row_factor = row_factor * factor

    largest = jnp.zeros((ROWS, 128), F32)
    for k in range(TILES):
        cols = pl.ds(128 * k, 128)
        update = g_buf[:, cols] * row_factor * root_col[k : k + 1]
        new_master = m_buf[:, cols] - learn_rate * update
        up_out[:, cols] = update
        nm_out[:, cols] = new_master
        largest = jnp.maximum(largest, jnp.abs(new_master))
    core_m[0] = jnp.max(largest, axis=0, keepdims=True)
    core_m_copy = remote(core_m.at[0], core_m.at[1], core_send.at[2], core_recv.at[2], mate)
    core_m_copy.start()
    codes_out[d] = jnp.clip(nm_out[...] * scale[:, 0:1], -code_limit, code_limit).astype(jnp.bfloat16)
    core_m_copy.wait_recv()
    z_m[z_mine] = jnp.maximum(core_m[0], core_m[1])
    group_start(z_m, z_mine, z_peers, 4)

    top, bottom = pl.ds(0, HALF), pl.ds(HALF, HALF)
    to_right = [
        remote(codes_out.at[d, part], codes_out.at[d, part], ag_send.at[i], ag_recv.at[i], right)
        for i, part in enumerate((top, bottom))
    ]
    to_left = [
        remote(codes_out.at[d, part], codes_out.at[d, part], ag_send.at[2 + i], ag_recv.at[2 + i], left)
        for i, part in enumerate((bottom, top))
    ]
    for i in range(2):
        to_right[i].start()
        to_left[i].start()
    to_right[0].wait_recv()
    on_right = remote(
        codes_out.at[dp_, top], codes_out.at[dp_, top], ag_send.at[4], ag_recv.at[4], right
    )
    on_right.start()
    to_left[0].wait_recv()
    on_left = remote(
        codes_out.at[dn, bottom], codes_out.at[dn, bottom], ag_send.at[5], ag_recv.at[5], left
    )
    on_left.start()

    def max_all(buf, n):
        total = buf[0]
        for k in range(1, n):
            total = jnp.maximum(total, buf[k])
        return total

    group_wait(z_m, z_peers, 4)
    xy_m[xy_mine] = max_all(z_m, len(z_peers) + 1)
    group_start(xy_m, xy_mine, xy_peers, 5)

    for a, b in first:
        a.wait_send()
        b.wait_send()
    plain_r.wait_send()
    plain_l.wait_send()
    for m, n in merged:
        m.wait_send()
        n.wait_send()
    core_c_copy.wait_send()
    core_s_copy.wait_send()
    core_m_copy.wait_send()
    group_done(xz_r, xz_peers, 0)
    group_done(yz_c, yz_peers, 1)
    group_done(xz_t, xz_peers, 2)
    group_done(yz_s, yz_peers, 3)
    group_done(z_m, z_peers, 4)
    to_right[1].wait_recv()
    to_left[1].wait_recv()
    on_right.wait_recv()
    on_left.wait_recv()
    group_wait(xy_m, xy_peers, 5)
    newest = jnp.max(max_all(xy_m, len(xy_peers) + 1), axis=1, keepdims=True)
    tail_out[0:1] = jnp.where(lane == 15, newest, shifted)
    for cp in (*to_right, *to_left, on_right, on_left):
        cp.wait_send()
    group_done(xy_m, xy_peers, 5)


def finish_kernel(
    nm_in, up_in, codes_in, row_in, col_in, tail,
    nm_out, up_out, row_out, col_out, codes_out, history_out, mean_out, last, mean, sems,
):
    copies = [
        pltpu.make_async_copy(a, b, sems.at[i])
        for i, (a, b) in enumerate(
            (
                (codes_in, codes_out),
                (nm_in, nm_out),
                (up_in, up_out),
                (row_in, row_out),
                (col_in, col_out),
                (last, history_out),
                (mean, mean_out),
            )
        )
    ]
    for cp in copies[:5]:
        cp.start()
    last[...] = tail[0, 0:16]
    mean[...] = tail[1, 0:1]
    for cp in copies[5:]:
        cp.start()
    for cp in copies:
        cp.wait()


def body(sizes, grad, master, row_prev, col_prev, history):
    n_dp, n_row, n_col = sizes
    n_yz = n_dp * n_row // 2
    n_x = min(n_col, 4)
    bf = jnp.bfloat16
    anywhere = pl.BlockSpec(memory_space=pl.ANY)
    vmem = pl.BlockSpec(memory_space=pltpu.VMEM)
    hbm = pl.BlockSpec(memory_space=pltpu.HBM)
    block = jax.ShapeDtypeStruct((ROWS, COLS), F32)
    codes = jax.ShapeDtypeStruct((n_dp, ROWS, COLS), bf)
    V = pltpu.VMEM
    dma = pltpu.SemaphoreType.DMA
    row_like, col_like = jax.ShapeDtypeStruct((1, ROWS), F32), jax.ShapeDtypeStruct((COLS,), F32)
    given = [pltpu.with_memory_space_constraint(a, pltpu.HBM) for a in (grad, master, row_prev, col_prev, history)]
    new_master, update, coded, row_new, col_new, tail = pl.pallas_call(
        functools.partial(step_kernel, sizes),
        out_shape=[block, block, codes, row_like, col_like, jax.ShapeDtypeStruct((8, 128), F32)],
        in_specs=[hbm] * 5,
        out_specs=[vmem] * 6,
        scratch_shapes=[
            V((HALF, COLS), bf), V((HALF, COLS), bf),
            V((ROWS, COLS), bf), V((ROWS, COLS), bf), V((ROWS, COLS), bf),
            V((HALF, COLS), bf), V((HALF, COLS), bf), V((HALF, COLS), bf), V((HALF, COLS), bf),
            V((ROWS, COLS), F32), V((ROWS, COLS), F32), V((ROWS, 128), F32), V((1, 128), F32), V((COLS,), F32), pltpu.SMEM((16,), F32),
            V((2, 8, 128), F32), V((n_yz, 8, 128), F32),
            V((n_col, 1, 128), F32), V((n_col, 1, 128), F32),
            V((2, 2, 128), F32), V((n_yz, 2, 128), F32),
            V((n_col // n_x * n_row // 2, 1, 128), F32), V((2, 1, 128), F32), V((n_dp * n_x, 1, 128), F32),
            dma((10,)), dma((10,)), dma((8,)), dma((3,)), dma((3,)), dma((6,)), dma((6,)), dma((6,)), dma((6,)),
            pltpu.SemaphoreType.REGULAR((2,)),
        ],
        compiler_params=pltpu.CompilerParams(
            collective_id=0, has_side_effects=True, vmem_limit_bytes=16 * 1024 * 1024
        ),
        name="step",
    )(*given)
    new_master, update, row_new, col_new, coded, new_history, row_mean = pl.pallas_call(
        finish_kernel,
        out_shape=[
            block, block, row_like, col_like, codes,
            jax.ShapeDtypeStruct((16,), F32), jax.ShapeDtypeStruct((1,), F32),
        ],
        in_specs=[anywhere] * 5 + [vmem],
        out_specs=[hbm] * 7,
        scratch_shapes=[V((16,), F32), V((1,), F32), dma((7,))],
        compiler_params=pltpu.CompilerParams(vmem_limit_bytes=1024 * 1024),
        name="finish",
    )(new_master, update, coded, row_new, col_new, tail)
    return (
        new_master[None], update[None], row_new, col_new, coded, new_history, row_mean.reshape(()),
    )


def solution(mesh):
    sizes = tuple(mesh.shape[a] for a in ("dp", "row", "col"))
    placed = (P("dp", None, "row", "col"), P("dp", "row", "col"), P("dp", "row"), P("col"), P())
    return jax.shard_map(
        functools.partial(body, sizes),
        mesh=mesh,
        in_specs=placed,
        out_specs=(
            P("dp", "row", "col"),
            P("dp", "row", "col"),
            P("dp", "row"),
            P("col"),
            P(None, "row", "col"),
            P(),
            P(),
        ),
        check_vma=False,
    )
```

```python
import functools

import jax
import jax.numpy as jnp
from jax import lax
from jax.experimental import pallas as pl
from jax.experimental.pallas import tpu as pltpu
from jax.sharding import PartitionSpec as P

MESH = pl.DeviceIdType.MESH
F32 = jnp.float32

decay_rate = 0.9
epsilon = 1e-30
learn_rate = 0.01
clip_limit = 1.0
code_limit = 4.0

ROWS, COLS = 128, 1024
HALF = ROWS // 2
CHUNK = 32
EARLY = 64
LATE = ROWS - EARLY
TILES = COLS // 128


def whole_wait(view, sem):
    pltpu.make_async_copy(view, view, sem).wait()


def far_first(n):
    return sorted(range(n), key=lambda k: -min(k, n - k))


def step_kernel(
    sizes, grad, master, row_prev, col_prev, history,
    nm_out, up_out, codes_out, row_out, col_out, tail_out,
    merge_r, merge_l, from_l, from_r, own, next_own, prev_own, sum_r, sum_l,
    g_buf, m_buf, rowp, rm_buf, cm_buf, old,
    core_c, yz_c, xz_r, xz_t, core_s, yz_s, z_m, core_m, xy_m,
    rs_send, rs_recv, loc, core_send, core_recv, grp_send, grp_recv, ag_send, ag_recv, greet, masters, steps,
):
    n_dp, n_row, n_col = sizes
    n_zl = n_row // 2
    n_yz = n_dp * n_zl
    total_rows, total_cols = n_dp * n_row * ROWS, n_col * COLS
    d, r, c = lax.axis_index("dp"), lax.axis_index("row"), lax.axis_index("col")
    n_x = min(n_col, 4)
    n_zh = n_col // n_x
    zl, core = r // 2, r % 2
    zh, x = c // n_x, c % n_x
    q = d * n_zl + zl
    dn, dp_, do = lax.rem(d + 1, n_dp), lax.rem(d + n_dp - 1, n_dp), lax.rem(d + 2, n_dp)
    right, left = (dn, r, c), (dp_, r, c)
    mate = (d, zl * 2 + (1 - core), c)
    yz_peers = [
        (lax.rem(d + i, n_dp), lax.rem(zl + j, n_zl) * 2 + core, c)
        for i in far_first(n_dp)
        for j in far_first(n_zl)
        if i or j
    ]
    xz_peers = [
        (d, r, lax.rem(zh + i, n_zh) * n_x + lax.rem(x + j, n_x))
        for i in far_first(n_zh)
        for j in far_first(n_x)
        if i or j
    ]
    z_near = [
        (d, r, lax.rem(zh + i, n_zh) * n_x + x) for i in sorted({1 % n_zh, n_zh - 1} - {0})
    ]
    near = [(lax.rem(d + i, n_dp), r, c) for i in far_first(n_dp) if i]
    near += [(d, lax.rem(zl + j, n_zl) * 2 + core, c) for j in far_first(n_zl) if j]
    near += [(d, r, zh * n_x + lax.rem(x + j, n_x)) for j in far_first(n_x) if j]
    near += z_near
    contacts = [*near, mate]
    z_peers = [
        (d, lax.rem(zl + j, n_zl) * 2 + core, lax.rem(zh + i, n_zh) * n_x + x)
        for i in far_first(n_zh)
        for j in far_first(n_zl)
        if i or j
    ]
    xy_peers = [
        (lax.rem(d + i, n_dp), r, zh * n_x + lax.rem(x + j, n_x))
        for i in far_first(n_dp)
        for j in far_first(n_x)
        if i or j
    ]
    dp_peers = [(lax.rem(d + i, n_dp), r, c) for i in far_first(n_dp) if i]
    z_mine, xy_mine = zh * n_zl + zl, d * n_x + x

    def remote(src, dst, send, recv, to):
        return pltpu.make_async_remote_copy(
            src, dst, send, recv, device_id=to, device_id_type=MESH
        )

    loads = [
        pltpu.make_async_copy(grad.at[0, d], own, loc.at[0]),
        pltpu.make_async_copy(grad.at[0, dn, pl.ds(0, HALF)], next_own, loc.at[1]),
        pltpu.make_async_copy(grad.at[0, dp_, pl.ds(HALF, HALF)], prev_own, loc.at[2]),
        pltpu.make_async_copy(master.at[0], m_buf, loc.at[3]),
        pltpu.make_async_copy(row_prev, rm_buf, loc.at[4]),
        pltpu.make_async_copy(col_prev, cm_buf, loc.at[5]),
        pltpu.make_async_copy(history, old, loc.at[6]),
    ]

    barrier = pltpu.get_barrier_semaphore()
    for p in contacts:
        pl.semaphore_signal(barrier, inc=1, device_id=p, device_id_type=MESH)
    for cp in loads:
        cp.start()
    pl.semaphore_wait(barrier, len(contacts))

    n_half = HALF // CHUNK
    sends = []
    first = []
    for i in range(n_half):
        lo, hi = pl.ds(CHUNK * i, CHUNK), pl.ds(HALF + CHUNK * i, CHUNK)
        here = pl.ds(CHUNK * i, CHUNK)
        a = remote(grad.at[0, do, lo], merge_r.at[here], rs_send.at[i], rs_recv.at[i], right)
        b = remote(grad.at[0, do, hi], merge_l.at[here], rs_send.at[2 + i], rs_recv.at[2 + i], left)
        a.start()
        b.start()
        first.append((a, b))
    plain_r = remote(
        grad.at[0, dn, pl.ds(HALF, HALF)], from_l.at[pl.ds(HALF, HALF)], rs_send.at[4], rs_recv.at[4], right
    )
    plain_l = remote(
        grad.at[0, dp_, pl.ds(0, HALF)], from_r.at[pl.ds(0, HALF)], rs_send.at[5], rs_recv.at[5], left
    )
    plain_r.start()
    plain_l.start()
    for p in near:
        pl.semaphore_signal(greet.at[0], inc=1, device_id=p, device_id_type=MESH)
    loads[3].wait()
    masters[d] = m_buf[pl.ds(LATE, EARLY)].astype(jnp.bfloat16)
    loads[1].wait()
    loads[2].wait()
    merged = []
    for i in range(n_half):
        here, hi = pl.ds(CHUNK * i, CHUNK), pl.ds(HALF + CHUNK * i, CHUNK)
        a, b = first[i]
        a.wait_recv()
        sum_r[here] = (next_own[here].astype(F32) + merge_r[here].astype(F32)).astype(jnp.bfloat16)
        m = remote(sum_r.at[here], from_l.at[here], rs_send.at[6 + i], rs_recv.at[6 + i], right)
        m.start()
        b.wait_recv()
        sum_l[here] = (prev_own[here].astype(F32) + merge_l[here].astype(F32)).astype(jnp.bfloat16)
        n = remote(sum_l.at[here], from_r.at[hi], rs_send.at[8 + i], rs_recv.at[8 + i], left)
        n.start()
        merged.append((m, n))

    pl.semaphore_wait(greet.at[0], len(near))
    for p in z_near:
        pl.semaphore_signal(greet.at[1], inc=1, device_id=p, device_id_type=MESH)
    loads[0].wait()
    plain_r.wait_recv()
    plain_l.wait_recv()
    col_sum = jnp.zeros((8, COLS), F32)
    for i in range(n_half):
        m, n = merged[i]
        for half, cp in ((0, m), (1, n)):
            cp.wait_recv()
            rows = pl.ds(HALF * half + CHUNK * i, CHUNK)
            g = own[rows].astype(F32) + from_l[rows].astype(F32) + from_r[rows].astype(F32)
            g_buf[rows] = g
            square = g * g + epsilon
            for j in range(CHUNK // 8):
                col_sum = col_sum + square[8 * j : 8 * j + 8]
            lanes = square[:, 0:128]
            for k in range(1, TILES):
                lanes = lanes + square[:, 128 * k : 128 * k + 128]
            rowp[rows] = lanes

    flat = jnp.sum(col_sum, axis=0, keepdims=True)
    packed = jnp.concatenate([flat[:, 128 * k : 128 * k + 128] for k in range(TILES)], axis=0)
    core_c[0] = packed
    core_c_copy = remote(core_c.at[0], core_c.at[1], core_send.at[0], core_recv.at[0], mate)
    core_c_copy.start()

    def group_start(buf, mine, peers, i):
        for p in peers:
            remote(buf.at[mine], buf.at[mine], grp_send.at[i], grp_recv.at[i], p).start()

    def group_wait(buf, peers, i):
        whole_wait(buf.at[pl.ds(0, len(peers))], grp_recv.at[i])

    def group_done(buf, peers, i):
        whole_wait(buf.at[pl.ds(0, len(peers))], grp_send.at[i])

    def block_start(buf, i):
        for p in dp_peers:
            remote(buf.at[d], buf.at[d], ag_send.at[i], ag_recv.at[i], p).start()

    def block_wait(i):
        whole_wait(masters.at[pl.ds(0, n_dp - 1)], ag_recv.at[i])

    def block_done(i):
        whole_wait(masters.at[pl.ds(0, n_dp - 1)], ag_send.at[i])

    def add_all(buf, n):
        total = buf[0]
        for k in range(1, n):
            total = total + buf[k]
        return total

    def lanes_to_row(values):
        return jnp.sum(values.T, axis=0, keepdims=True)

    def row_to_lanes(values):
        return jnp.broadcast_to(values, (128, 128)).T

    xz_r[c] = lanes_to_row(rowp[...])
    if z_near:
        pl.semaphore_wait(greet.at[1], len(z_near))
    group_start(xz_r, c, xz_peers, 0)
    core_c_copy.wait_recv()
    yz_c[q] = core_c[0] + core_c[1]
    group_start(yz_c, q, yz_peers, 1)
    block_start(masters, 0)
    loads[4].wait()
    loads[5].wait()
    group_wait(yz_c, yz_peers, 1)
    col_total = add_all(yz_c, n_yz)
    col_old = jnp.concatenate(
        [cm_buf[pl.ds(128 * k, 128)].reshape(1, 128) for k in range(TILES)], axis=0
    )
    col_new = decay_rate * col_old + (1.0 - decay_rate) * (col_total / total_rows)
    for k in range(TILES):
        col_out[pl.ds(128 * k, 128)] = col_new[k]
    inv_col = 1.0 / col_new
    root_col = 1.0 / jnp.sqrt(col_new)

    lanes = jnp.zeros((ROWS, 128), F32)
    for k in range(TILES):
        g = g_buf[:, pl.ds(128 * k, 128)]
        lanes = lanes + g * g * inv_col[k : k + 1]
    xz_t[c] = lanes_to_row(lanes)
    group_start(xz_t, c, xz_peers, 2)
    group_wait(xz_r, xz_peers, 0)
    row_total = add_all(xz_r, n_col)
    row_new = decay_rate * rm_buf[...] + (1.0 - decay_rate) * (row_total / total_cols)
    row_out[...] = row_new
    row_factor = row_to_lanes(1.0 / jnp.sqrt(row_new))
    for k in range(TILES):
        cols = pl.ds(128 * k, 128)
        step = g_buf[:, cols] * row_factor * root_col[k : k + 1]
        g_buf[:, cols] = step
        steps[d, :, cols] = step[LATE:].astype(jnp.bfloat16)
    block_start(steps, 1)
    group_wait(xz_t, xz_peers, 2)
    weighted = add_all(xz_t, n_col) / row_new

    core_s[0] = jnp.concatenate([weighted, row_new], axis=0)
    core_s_copy = remote(core_s.at[0], core_s.at[1], core_send.at[1], core_recv.at[1], mate)
    core_s_copy.start()
    core_s_copy.wait_recv()
    yz_s[q] = core_s[0] + core_s[1]
    group_start(yz_s, q, yz_peers, 3)
    loads[6].wait()
    largest_old = old[0]
    for i in range(1, 16):
        largest_old = jnp.maximum(largest_old, old[i])
    lane = lax.broadcasted_iota(jnp.int32, (1, 128), 1)
    shifted = jnp.zeros((1, 128), F32)
    for i in range(15):
        shifted = jnp.where(lane == i, old[i + 1], shifted)
    scale = code_limit / jnp.full((1, 128), largest_old, F32)
    group_wait(yz_s, yz_peers, 3)
    totals = jnp.sum(add_all(yz_s, n_yz), axis=1, keepdims=True)
    row_mean = totals[1:2] / total_rows
    step_rms = jnp.sqrt(row_mean * totals[0:1] / (float(total_rows) * float(total_cols)))
    factor = jnp.sqrt(row_mean) / jnp.maximum(1.0, step_rms / clip_limit)
    tail_out[1:2] = jnp.broadcast_to(row_mean, (1, 128))
    tail_out[2:8] = jnp.zeros((6, 128), F32)

    largest = jnp.zeros((ROWS, 128), F32)
    for k in range(TILES):
        cols = pl.ds(128 * k, 128)
        update = g_buf[:, cols] * factor
        new_master = m_buf[:, cols] - learn_rate * update
        up_out[:, cols] = update
        nm_out[:, cols] = new_master
        largest = jnp.maximum(largest, jnp.abs(new_master))
    core_m[0] = jnp.max(largest, axis=0, keepdims=True)
    core_m_copy = remote(core_m.at[0], core_m.at[1], core_send.at[2], core_recv.at[2], mate)
    core_m_copy.start()
    core_m_copy.wait_recv()
    z_m[z_mine] = jnp.maximum(core_m[0], core_m[1])
    group_start(z_m, z_mine, z_peers, 4)

    top, bottom = pl.ds(0, LATE // 2), pl.ds(LATE // 2, LATE // 2)
    codes_out[d, pl.ds(0, LATE)] = jnp.clip(nm_out[pl.ds(0, LATE)] * scale[:, 0:1], -code_limit, code_limit).astype(
        jnp.bfloat16
    )
    to_right = [
        remote(codes_out.at[d, part], codes_out.at[d, part], ag_send.at[2 + i], ag_recv.at[2 + i], right)
        for i, part in enumerate((top, bottom))
    ]
    to_left = [
        remote(codes_out.at[d, part], codes_out.at[d, part], ag_send.at[4 + i], ag_recv.at[4 + i], left)
        for i, part in enumerate((bottom, top))
    ]
    for i in range(2):
        to_right[i].start()
        to_left[i].start()

    block_wait(0)
    block_wait(1)
    rate = learn_rate * factor
    for j in range(n_dp):
        moved = masters[j].astype(F32) - rate * steps[j].astype(F32)
        codes_out[j, pl.ds(LATE, EARLY)] = jnp.clip(moved * scale[:, 0:1], -code_limit, code_limit).astype(jnp.bfloat16)
    to_right[0].wait_recv()
    on_right = remote(
        codes_out.at[dp_, top], codes_out.at[dp_, top], ag_send.at[6], ag_recv.at[6], right
    )
    on_right.start()
    to_left[0].wait_recv()
    on_left = remote(
        codes_out.at[dn, bottom], codes_out.at[dn, bottom], ag_send.at[7], ag_recv.at[7], left
    )
    on_left.start()

    def max_all(buf, n):
        total = buf[0]
        for k in range(1, n):
            total = jnp.maximum(total, buf[k])
        return total

    group_wait(z_m, z_peers, 4)
    xy_m[xy_mine] = max_all(z_m, len(z_peers) + 1)
    group_start(xy_m, xy_mine, xy_peers, 5)

    for a, b in first:
        a.wait_send()
        b.wait_send()
    plain_r.wait_send()
    plain_l.wait_send()
    for m, n in merged:
        m.wait_send()
        n.wait_send()
    core_c_copy.wait_send()
    core_s_copy.wait_send()
    core_m_copy.wait_send()
    group_done(xz_r, xz_peers, 0)
    group_done(yz_c, yz_peers, 1)
    group_done(xz_t, xz_peers, 2)
    group_done(yz_s, yz_peers, 3)
    group_done(z_m, z_peers, 4)
    to_right[1].wait_recv()
    to_left[1].wait_recv()
    on_right.wait_recv()
    on_left.wait_recv()
    group_wait(xy_m, xy_peers, 5)
    newest = jnp.max(max_all(xy_m, len(xy_peers) + 1), axis=1, keepdims=True)
    tail_out[0:1] = jnp.where(lane == 15, newest, shifted)
    for cp in (*to_right, *to_left, on_right, on_left):
        cp.wait_send()
    block_done(0)
    block_done(1)
    group_done(xy_m, xy_peers, 5)


def finish_kernel(
    nm_in, up_in, codes_in, row_in, col_in, tail,
    nm_out, up_out, row_out, col_out, codes_out, history_out, mean_out, last, mean, sems,
):
    copies = [
        pltpu.make_async_copy(a, b, sems.at[i])
        for i, (a, b) in enumerate(
            (
                (codes_in, codes_out),
                (nm_in, nm_out),
                (up_in, up_out),
                (row_in, row_out),
                (col_in, col_out),
                (last, history_out),
                (mean, mean_out),
            )
        )
    ]
    for cp in copies[:5]:
        cp.start()
    last[...] = tail[0, 0:16]
    mean[...] = tail[1, 0:1]
    for cp in copies[5:]:
        cp.start()
    for cp in copies:
        cp.wait()


def body(sizes, grad, master, row_prev, col_prev, history):
    n_dp, n_row, n_col = sizes
    n_yz = n_dp * n_row // 2
    n_x = min(n_col, 4)
    bf = jnp.bfloat16
    anywhere = pl.BlockSpec(memory_space=pl.ANY)
    vmem = pl.BlockSpec(memory_space=pltpu.VMEM)
    hbm = pl.BlockSpec(memory_space=pltpu.HBM)
    block = jax.ShapeDtypeStruct((ROWS, COLS), F32)
    codes = jax.ShapeDtypeStruct((n_dp, ROWS, COLS), bf)
    V = pltpu.VMEM
    dma = pltpu.SemaphoreType.DMA
    row_like, col_like = jax.ShapeDtypeStruct((1, ROWS), F32), jax.ShapeDtypeStruct((COLS,), F32)
    given = [pltpu.with_memory_space_constraint(a, pltpu.HBM) for a in (grad, master, row_prev, col_prev, history)]
    new_master, update, coded, row_new, col_new, tail = pl.pallas_call(
        functools.partial(step_kernel, sizes),
        out_shape=[block, block, codes, row_like, col_like, jax.ShapeDtypeStruct((8, 128), F32)],
        in_specs=[hbm] * 5,
        out_specs=[vmem] * 6,
        scratch_shapes=[
            V((HALF, COLS), bf), V((HALF, COLS), bf),
            V((ROWS, COLS), bf), V((ROWS, COLS), bf), V((ROWS, COLS), bf),
            V((HALF, COLS), bf), V((HALF, COLS), bf), V((HALF, COLS), bf), V((HALF, COLS), bf),
            V((ROWS, COLS), F32), V((ROWS, COLS), F32), V((ROWS, 128), F32), V((1, 128), F32), V((COLS,), F32), pltpu.SMEM((16,), F32),
            V((2, 8, 128), F32), V((n_yz, 8, 128), F32),
            V((n_col, 1, 128), F32), V((n_col, 1, 128), F32),
            V((2, 2, 128), F32), V((n_yz, 2, 128), F32),
            V((n_col // n_x * n_row // 2, 1, 128), F32), V((2, 1, 128), F32), V((n_dp * n_x, 1, 128), F32),
            dma((10,)), dma((10,)), dma((8,)), dma((3,)), dma((3,)), dma((6,)), dma((6,)), dma((8,)), dma((8,)),
            pltpu.SemaphoreType.REGULAR((2,)), V((n_dp, EARLY, COLS), bf), V((n_dp, EARLY, COLS), bf),
        ],
        compiler_params=pltpu.CompilerParams(
            collective_id=0, has_side_effects=True, vmem_limit_bytes=16 * 1024 * 1024
        ),
        name="step",
    )(*given)
    new_master, update, row_new, col_new, coded, new_history, row_mean = pl.pallas_call(
        finish_kernel,
        out_shape=[
            block, block, row_like, col_like, codes,
            jax.ShapeDtypeStruct((16,), F32), jax.ShapeDtypeStruct((1,), F32),
        ],
        in_specs=[anywhere] * 5 + [vmem],
        out_specs=[hbm] * 7,
        scratch_shapes=[V((16,), F32), V((1,), F32), dma((7,))],
        compiler_params=pltpu.CompilerParams(vmem_limit_bytes=1024 * 1024),
        name="finish",
    )(new_master, update, coded, row_new, col_new, tail)
    return (
        new_master[None], update[None], row_new, col_new, coded, new_history, row_mean.reshape(()),
    )


def solution(mesh):
    sizes = tuple(mesh.shape[a] for a in ("dp", "row", "col"))
    placed = (P("dp", None, "row", "col"), P("dp", "row", "col"), P("dp", "row"), P("col"), P())
    return jax.shard_map(
        functools.partial(body, sizes),
        mesh=mesh,
        in_specs=placed,
        out_specs=(
            P("dp", "row", "col"),
            P("dp", "row", "col"),
            P("dp", "row"),
            P("col"),
            P(None, "row", "col"),
            P(),
            P(),
        ),
        check_vma=False,
    )
```

```python
import functools

import jax
import jax.numpy as jnp
from jax import lax
from jax.experimental import pallas as pl
from jax.experimental.pallas import tpu as pltpu
from jax.sharding import PartitionSpec as P

MESH = pl.DeviceIdType.MESH
F32 = jnp.float32

decay_rate = 0.9
epsilon = 1e-30
learn_rate = 0.01
clip_limit = 1.0
code_limit = 4.0

ROWS, COLS = 128, 1024
HALF = ROWS // 2
CHUNK = 32
EARLY = 64
LATE = ROWS - EARLY
TILES = COLS // 128


def whole_wait(view, sem):
    pltpu.make_async_copy(view, view, sem).wait()


def far_first(n):
    return sorted(range(n), key=lambda k: -min(k, n - k))


def step_kernel(
    sizes, grad, master, row_prev, col_prev, history,
    nm_out, up_out, codes_out, row_out, col_out, tail_out,
    merge_r, merge_l, from_l, from_r, own, next_own, prev_own, sum_r, sum_l,
    g_buf, m_buf, rowp, rm_buf, cm_buf, old,
    core_c, yz_c, xz_r, xz_t, core_s, yz_s, z_m, core_m, xy_m,
    rs_send, rs_recv, loc, core_send, core_recv, grp_send, grp_recv, ag_send, ag_recv, greet, masters, steps,
):
    n_dp, n_row, n_col = sizes
    n_zl = n_row // 2
    n_yz = n_dp * n_zl
    total_rows, total_cols = n_dp * n_row * ROWS, n_col * COLS
    d, r, c = lax.axis_index("dp"), lax.axis_index("row"), lax.axis_index("col")
    n_x = min(n_col, 4)
    n_zh = n_col // n_x
    zl, core = r // 2, r % 2
    zh, x = c // n_x, c % n_x
    q = d * n_zl + zl
    dn, dp_, do = lax.rem(d + 1, n_dp), lax.rem(d + n_dp - 1, n_dp), lax.rem(d + 2, n_dp)
    right, left = (dn, r, c), (dp_, r, c)
    mate = (d, zl * 2 + (1 - core), c)
    yz_peers = [
        (lax.rem(d + i, n_dp), lax.rem(zl + j, n_zl) * 2 + core, c)
        for i in far_first(n_dp)
        for j in far_first(n_zl)
        if i or j
    ]
    xz_peers = [
        (d, r, lax.rem(zh + i, n_zh) * n_x + lax.rem(x + j, n_x))
        for i in far_first(n_zh)
        for j in far_first(n_x)
        if i or j
    ]
    z_near = [
        (d, r, lax.rem(zh + i, n_zh) * n_x + x) for i in sorted({1 % n_zh, n_zh - 1} - {0})
    ]
    near = [(lax.rem(d + i, n_dp), r, c) for i in far_first(n_dp) if i]
    near += [(d, lax.rem(zl + j, n_zl) * 2 + core, c) for j in far_first(n_zl) if j]
    near += [(d, r, zh * n_x + lax.rem(x + j, n_x)) for j in far_first(n_x) if j]
    near += z_near
    contacts = [*near, mate]
    z_peers = [
        (d, lax.rem(zl + j, n_zl) * 2 + core, lax.rem(zh + i, n_zh) * n_x + x)
        for i in far_first(n_zh)
        for j in far_first(n_zl)
        if i or j
    ]
    xy_peers = [
        (lax.rem(d + i, n_dp), r, zh * n_x + lax.rem(x + j, n_x))
        for i in far_first(n_dp)
        for j in far_first(n_x)
        if i or j
    ]
    dp_peers = [(lax.rem(d + i, n_dp), r, c) for i in far_first(n_dp) if i]
    z_mine, xy_mine = zh * n_zl + zl, d * n_x + x

    def remote(src, dst, send, recv, to):
        return pltpu.make_async_remote_copy(
            src, dst, send, recv, device_id=to, device_id_type=MESH
        )

    loads = [
        pltpu.make_async_copy(grad.at[0, d], own, loc.at[0]),
        pltpu.make_async_copy(grad.at[0, dn, pl.ds(0, HALF)], next_own, loc.at[1]),
        pltpu.make_async_copy(grad.at[0, dp_, pl.ds(HALF, HALF)], prev_own, loc.at[2]),
        pltpu.make_async_copy(master.at[0], m_buf, loc.at[3]),
        pltpu.make_async_copy(row_prev, rm_buf, loc.at[4]),
        pltpu.make_async_copy(col_prev, cm_buf, loc.at[5]),
        pltpu.make_async_copy(history, old, loc.at[6]),
    ]

    barrier = pltpu.get_barrier_semaphore()
    for p in contacts:
        pl.semaphore_signal(barrier, inc=1, device_id=p, device_id_type=MESH)
    for cp in loads:
        cp.start()
    pl.semaphore_wait(barrier, len(contacts))

    n_half = HALF // CHUNK
    sends = []
    first = []
    for i in range(n_half):
        lo, hi = pl.ds(CHUNK * i, CHUNK), pl.ds(HALF + CHUNK * i, CHUNK)
        here = pl.ds(CHUNK * i, CHUNK)
        a = remote(grad.at[0, do, lo], merge_r.at[here], rs_send.at[i], rs_recv.at[i], right)
        b = remote(grad.at[0, do, hi], merge_l.at[here], rs_send.at[2 + i], rs_recv.at[2 + i], left)
        a.start()
        b.start()
        first.append((a, b))
    plain_r = remote(
        grad.at[0, dn, pl.ds(HALF, HALF)], from_l.at[pl.ds(HALF, HALF)], rs_send.at[4], rs_recv.at[4], right
    )
    plain_l = remote(
        grad.at[0, dp_, pl.ds(0, HALF)], from_r.at[pl.ds(0, HALF)], rs_send.at[5], rs_recv.at[5], left
    )
    plain_r.start()
    plain_l.start()
    for p in near:
        pl.semaphore_signal(greet.at[0], inc=1, device_id=p, device_id_type=MESH)
    loads[3].wait()
    masters[d] = m_buf[pl.ds(LATE, EARLY)].astype(jnp.bfloat16)
    loads[1].wait()
    loads[2].wait()
    merged = []
    for i in range(n_half):
        here, hi = pl.ds(CHUNK * i, CHUNK), pl.ds(HALF + CHUNK * i, CHUNK)
        a, b = first[i]
        a.wait_recv()
        sum_r[here] = (next_own[here].astype(F32) + merge_r[here].astype(F32)).astype(jnp.bfloat16)
        m = remote(sum_r.at[here], from_l.at[here], rs_send.at[6 + i], rs_recv.at[6 + i], right)
        m.start()
        b.wait_recv()
        sum_l[here] = (prev_own[here].astype(F32) + merge_l[here].astype(F32)).astype(jnp.bfloat16)
        n = remote(sum_l.at[here], from_r.at[hi], rs_send.at[8 + i], rs_recv.at[8 + i], left)
        n.start()
        merged.append((m, n))

    pl.semaphore_wait(greet.at[0], len(near))
    for p in z_near:
        pl.semaphore_signal(greet.at[1], inc=1, device_id=p, device_id_type=MESH)
    loads[0].wait()
    plain_r.wait_recv()
    plain_l.wait_recv()
    col_sum = jnp.zeros((8, COLS), F32)
    for i in range(n_half):
        m, n = merged[i]
        for half, cp in ((0, m), (1, n)):
            cp.wait_recv()
            rows = pl.ds(HALF * half + CHUNK * i, CHUNK)
            g = own[rows].astype(F32) + from_l[rows].astype(F32) + from_r[rows].astype(F32)
            g_buf[rows] = g
            square = g * g + epsilon
            for j in range(CHUNK // 8):
                col_sum = col_sum + square[8 * j : 8 * j + 8]
            lanes = square[:, 0:128]
            for k in range(1, TILES):
                lanes = lanes + square[:, 128 * k : 128 * k + 128]
            rowp[rows] = lanes

    flat = jnp.sum(col_sum, axis=0, keepdims=True)
    packed = jnp.concatenate([flat[:, 128 * k : 128 * k + 128] for k in range(TILES)], axis=0)
    core_c[0] = packed
    core_c_copy = remote(core_c.at[0], core_c.at[1], core_send.at[0], core_recv.at[0], mate)
    core_c_copy.start()

    def group_start(buf, mine, peers, i):
        for p in peers:
            remote(buf.at[mine], buf.at[mine], grp_send.at[i], grp_recv.at[i], p).start()

    def group_wait(buf, peers, i):
        whole_wait(buf.at[pl.ds(0, len(peers))], grp_recv.at[i])

    def group_done(buf, peers, i):
        whole_wait(buf.at[pl.ds(0, len(peers))], grp_send.at[i])

    def block_start(buf, i):
        for p in dp_peers:
            remote(buf.at[d], buf.at[d], ag_send.at[i], ag_recv.at[i], p).start()

    def block_wait(i):
        whole_wait(masters.at[pl.ds(0, n_dp - 1)], ag_recv.at[i])

    def block_done(i):
        whole_wait(masters.at[pl.ds(0, n_dp - 1)], ag_send.at[i])

    def add_all(buf, n):
        total = buf[0]
        for k in range(1, n):
            total = total + buf[k]
        return total

    def lanes_to_row(values):
        return jnp.sum(values.T, axis=0, keepdims=True)

    def row_to_lanes(values):
        return jnp.broadcast_to(values, (128, 128)).T

    xz_r[c] = lanes_to_row(rowp[...])
    if z_near:
        pl.semaphore_wait(greet.at[1], len(z_near))
    group_start(xz_r, c, xz_peers, 0)
    core_c_copy.wait_recv()
    yz_c[q] = core_c[0] + core_c[1]
    group_start(yz_c, q, yz_peers, 1)
    block_start(masters, 0)
    loads[4].wait()
    loads[5].wait()
    group_wait(yz_c, yz_peers, 1)
    col_total = add_all(yz_c, n_yz)
    col_old = jnp.concatenate(
        [cm_buf[pl.ds(128 * k, 128)].reshape(1, 128) for k in range(TILES)], axis=0
    )
    col_new = decay_rate * col_old + (1.0 - decay_rate) * (col_total / total_rows)
    for k in range(TILES):
        col_out[pl.ds(128 * k, 128)] = col_new[k]
    inv_col = 1.0 / col_new
    root_col = 1.0 / jnp.sqrt(col_new)

    lanes = jnp.zeros((ROWS, 128), F32)
    for k in range(TILES):
        g = g_buf[:, pl.ds(128 * k, 128)]
        lanes = lanes + g * g * inv_col[k : k + 1]
    xz_t[c] = lanes_to_row(lanes)
    group_start(xz_t, c, xz_peers, 2)
    group_wait(xz_r, xz_peers, 0)
    row_total = add_all(xz_r, n_col)
    row_new = decay_rate * rm_buf[...] + (1.0 - decay_rate) * (row_total / total_cols)
    row_out[...] = row_new
    row_factor = row_to_lanes(1.0 / jnp.sqrt(row_new))
    for k in range(TILES):
        cols = pl.ds(128 * k, 128)
        step = g_buf[:, cols] * row_factor * root_col[k : k + 1]
        g_buf[:, cols] = step
        steps[d, :, cols] = step[LATE:].astype(jnp.bfloat16)
    block_start(steps, 1)
    group_wait(xz_t, xz_peers, 2)
    weighted = add_all(xz_t, n_col) / row_new

    core_s[0] = jnp.concatenate([weighted, row_new], axis=0)
    core_s_copy = remote(core_s.at[0], core_s.at[1], core_send.at[1], core_recv.at[1], mate)
    core_s_copy.start()
    core_s_copy.wait_recv()
    yz_s[q] = core_s[0] + core_s[1]
    group_start(yz_s, q, yz_peers, 3)
    loads[6].wait()
    largest_old = old[0]
    for i in range(1, 16):
        largest_old = jnp.maximum(largest_old, old[i])
    lane = lax.broadcasted_iota(jnp.int32, (1, 128), 1)
    shifted = jnp.zeros((1, 128), F32)
    for i in range(15):
        shifted = jnp.where(lane == i, old[i + 1], shifted)
    scale = code_limit / jnp.full((1, 128), largest_old, F32)
    group_wait(yz_s, yz_peers, 3)
    totals = jnp.sum(add_all(yz_s, n_yz), axis=1, keepdims=True)
    row_mean = totals[1:2] / total_rows
    step_rms = jnp.sqrt(row_mean * totals[0:1] / (float(total_rows) * float(total_cols)))
    factor = jnp.sqrt(row_mean) / jnp.maximum(1.0, step_rms / clip_limit)
    tail_out[1:2] = jnp.broadcast_to(row_mean, (1, 128))
    tail_out[2:8] = jnp.zeros((6, 128), F32)

    rate = learn_rate * factor
    largest = jnp.zeros((ROWS, 128), F32)
    for k in range(TILES):
        cols = pl.ds(128 * k, 128)
        largest = jnp.maximum(largest, jnp.abs(m_buf[:, cols] - rate * g_buf[:, cols]))
    core_m[0] = jnp.max(largest, axis=0, keepdims=True)
    core_m_copy = remote(core_m.at[0], core_m.at[1], core_send.at[2], core_recv.at[2], mate)
    core_m_copy.start()
    for k in range(TILES):
        cols = pl.ds(128 * k, 128)
        update = g_buf[:, cols] * factor
        up_out[:, cols] = update
        nm_out[:, cols] = m_buf[:, cols] - learn_rate * update
    core_m_copy.wait_recv()
    z_m[z_mine] = jnp.maximum(core_m[0], core_m[1])
    group_start(z_m, z_mine, z_peers, 4)

    top, bottom = pl.ds(0, LATE // 2), pl.ds(LATE // 2, LATE // 2)
    codes_out[d, pl.ds(0, LATE)] = jnp.clip(nm_out[pl.ds(0, LATE)] * scale[:, 0:1], -code_limit, code_limit).astype(
        jnp.bfloat16
    )
    to_right = [
        remote(codes_out.at[d, part], codes_out.at[d, part], ag_send.at[2 + i], ag_recv.at[2 + i], right)
        for i, part in enumerate((top, bottom))
    ]
    to_left = [
        remote(codes_out.at[d, part], codes_out.at[d, part], ag_send.at[4 + i], ag_recv.at[4 + i], left)
        for i, part in enumerate((bottom, top))
    ]
    for i in range(2):
        to_right[i].start()
        to_left[i].start()

    to_right[0].wait_recv()
    on_right = remote(
        codes_out.at[dp_, top], codes_out.at[dp_, top], ag_send.at[6], ag_recv.at[6], right
    )
    on_right.start()
    to_left[0].wait_recv()
    on_left = remote(
        codes_out.at[dn, bottom], codes_out.at[dn, bottom], ag_send.at[7], ag_recv.at[7], left
    )
    on_left.start()

    def max_all(buf, n):
        total = buf[0]
        for k in range(1, n):
            total = jnp.maximum(total, buf[k])
        return total

    group_wait(z_m, z_peers, 4)
    xy_m[xy_mine] = max_all(z_m, len(z_peers) + 1)
    group_start(xy_m, xy_mine, xy_peers, 5)

    block_wait(0)
    block_wait(1)
    for j in range(n_dp):
        moved = masters[j].astype(F32) - rate * steps[j].astype(F32)
        codes_out[j, pl.ds(LATE, EARLY)] = jnp.clip(moved * scale[:, 0:1], -code_limit, code_limit).astype(jnp.bfloat16)

    for a, b in first:
        a.wait_send()
        b.wait_send()
    plain_r.wait_send()
    plain_l.wait_send()
    for m, n in merged:
        m.wait_send()
        n.wait_send()
    core_c_copy.wait_send()
    core_s_copy.wait_send()
    core_m_copy.wait_send()
    group_done(xz_r, xz_peers, 0)
    group_done(yz_c, yz_peers, 1)
    group_done(xz_t, xz_peers, 2)
    group_done(yz_s, yz_peers, 3)
    group_done(z_m, z_peers, 4)
    to_right[1].wait_recv()
    to_left[1].wait_recv()
    on_right.wait_recv()
    on_left.wait_recv()
    group_wait(xy_m, xy_peers, 5)
    newest = jnp.max(max_all(xy_m, len(xy_peers) + 1), axis=1, keepdims=True)
    tail_out[0:1] = jnp.where(lane == 15, newest, shifted)
    for cp in (*to_right, *to_left, on_right, on_left):
        cp.wait_send()
    block_done(0)
    block_done(1)
    group_done(xy_m, xy_peers, 5)


def finish_kernel(
    nm_in, up_in, codes_in, row_in, col_in, tail,
    nm_out, up_out, row_out, col_out, codes_out, history_out, mean_out, last, mean, sems,
):
    copies = [
        pltpu.make_async_copy(a, b, sems.at[i])
        for i, (a, b) in enumerate(
            (
                (codes_in, codes_out),
                (nm_in, nm_out),
                (up_in, up_out),
                (row_in, row_out),
                (col_in, col_out),
                (last, history_out),
                (mean, mean_out),
            )
        )
    ]
    for cp in copies[:5]:
        cp.start()
    last[...] = tail[0, 0:16]
    mean[...] = tail[1, 0:1]
    for cp in copies[5:]:
        cp.start()
    for cp in copies:
        cp.wait()


def body(sizes, grad, master, row_prev, col_prev, history):
    n_dp, n_row, n_col = sizes
    n_yz = n_dp * n_row // 2
    n_x = min(n_col, 4)
    bf = jnp.bfloat16
    anywhere = pl.BlockSpec(memory_space=pl.ANY)
    vmem = pl.BlockSpec(memory_space=pltpu.VMEM)
    hbm = pl.BlockSpec(memory_space=pltpu.HBM)
    block = jax.ShapeDtypeStruct((ROWS, COLS), F32)
    codes = jax.ShapeDtypeStruct((n_dp, ROWS, COLS), bf)
    V = pltpu.VMEM
    dma = pltpu.SemaphoreType.DMA
    row_like, col_like = jax.ShapeDtypeStruct((1, ROWS), F32), jax.ShapeDtypeStruct((COLS,), F32)
    given = [pltpu.with_memory_space_constraint(a, pltpu.HBM) for a in (grad, master, row_prev, col_prev, history)]
    new_master, update, coded, row_new, col_new, tail = pl.pallas_call(
        functools.partial(step_kernel, sizes),
        out_shape=[block, block, codes, row_like, col_like, jax.ShapeDtypeStruct((8, 128), F32)],
        in_specs=[hbm] * 5,
        out_specs=[vmem] * 6,
        scratch_shapes=[
            V((HALF, COLS), bf), V((HALF, COLS), bf),
            V((ROWS, COLS), bf), V((ROWS, COLS), bf), V((ROWS, COLS), bf),
            V((HALF, COLS), bf), V((HALF, COLS), bf), V((HALF, COLS), bf), V((HALF, COLS), bf),
            V((ROWS, COLS), F32), V((ROWS, COLS), F32), V((ROWS, 128), F32), V((1, 128), F32), V((COLS,), F32), pltpu.SMEM((16,), F32),
            V((2, 8, 128), F32), V((n_yz, 8, 128), F32),
            V((n_col, 1, 128), F32), V((n_col, 1, 128), F32),
            V((2, 2, 128), F32), V((n_yz, 2, 128), F32),
            V((n_col // n_x * n_row // 2, 1, 128), F32), V((2, 1, 128), F32), V((n_dp * n_x, 1, 128), F32),
            dma((10,)), dma((10,)), dma((8,)), dma((3,)), dma((3,)), dma((6,)), dma((6,)), dma((8,)), dma((8,)),
            pltpu.SemaphoreType.REGULAR((2,)), V((n_dp, EARLY, COLS), bf), V((n_dp, EARLY, COLS), bf),
        ],
        compiler_params=pltpu.CompilerParams(
            collective_id=0, has_side_effects=True, vmem_limit_bytes=16 * 1024 * 1024
        ),
        name="step",
    )(*given)
    new_master, update, row_new, col_new, coded, new_history, row_mean = pl.pallas_call(
        finish_kernel,
        out_shape=[
            block, block, row_like, col_like, codes,
            jax.ShapeDtypeStruct((16,), F32), jax.ShapeDtypeStruct((1,), F32),
        ],
        in_specs=[anywhere] * 5 + [vmem],
        out_specs=[hbm] * 7,
        scratch_shapes=[V((16,), F32), V((1,), F32), dma((7,))],
        compiler_params=pltpu.CompilerParams(vmem_limit_bytes=1024 * 1024),
        name="finish",
    )(new_master, update, coded, row_new, col_new, tail)
    return (
        new_master[None], update[None], row_new, col_new, coded, new_history, row_mean.reshape(()),
    )


def solution(mesh):
    sizes = tuple(mesh.shape[a] for a in ("dp", "row", "col"))
    placed = (P("dp", None, "row", "col"), P("dp", "row", "col"), P("dp", "row"), P("col"), P())
    return jax.shard_map(
        functools.partial(body, sizes),
        mesh=mesh,
        in_specs=placed,
        out_specs=(
            P("dp", "row", "col"),
            P("dp", "row", "col"),
            P("dp", "row"),
            P("col"),
            P(None, "row", "col"),
            P(),
            P(),
        ),
        check_vma=False,
    )
```

```python
import functools

import jax
import jax.numpy as jnp
from jax import lax
from jax.experimental import pallas as pl
from jax.experimental.pallas import tpu as pltpu
from jax.sharding import PartitionSpec as P

MESH = pl.DeviceIdType.MESH
F32 = jnp.float32

decay_rate = 0.9
epsilon = 1e-30
learn_rate = 0.01
clip_limit = 1.0
code_limit = 4.0

ROWS, COLS = 128, 1024
HALF = ROWS // 2
CHUNK = 32
EARLY = 64
LATE = ROWS - EARLY
TILES = COLS // 128


def whole_wait(view, sem):
    pltpu.make_async_copy(view, view, sem).wait()


def far_first(n):
    return sorted(range(n), key=lambda k: -min(k, n - k))


def step_kernel(
    sizes, grad, master, row_prev, col_prev, history,
    nm_out, up_out, codes_out, row_out, col_out, tail_out,
    merge_r, merge_l, from_l, from_r, own, next_own, prev_own, sum_r, sum_l,
    g_buf, m_buf, rowp, rm_buf, cm_buf, old,
    core_c, yz_c, xz_r, xz_t, core_s, yz_s, z_m, core_m, xy_m,
    rs_send, rs_recv, loc, core_send, core_recv, grp_send, grp_recv, ag_send, ag_recv, greet, masters, steps,
):
    n_dp, n_row, n_col = sizes
    n_zl = n_row // 2
    n_yz = n_dp * n_zl
    total_rows, total_cols = n_dp * n_row * ROWS, n_col * COLS
    d, r, c = lax.axis_index("dp"), lax.axis_index("row"), lax.axis_index("col")
    n_x = min(n_col, 4)
    n_zh = n_col // n_x
    zl, core = r // 2, r % 2
    zh, x = c // n_x, c % n_x
    q = d * n_zl + zl
    dn, dp_, do = lax.rem(d + 1, n_dp), lax.rem(d + n_dp - 1, n_dp), lax.rem(d + 2, n_dp)
    right, left = (dn, r, c), (dp_, r, c)
    mate = (d, zl * 2 + (1 - core), c)
    yz_peers = [
        (lax.rem(d + i, n_dp), lax.rem(zl + j, n_zl) * 2 + core, c)
        for i in far_first(n_dp)
        for j in far_first(n_zl)
        if i or j
    ]
    xz_peers = [
        (d, r, lax.rem(zh + i, n_zh) * n_x + lax.rem(x + j, n_x))
        for i in far_first(n_zh)
        for j in far_first(n_x)
        if i or j
    ]
    z_near = [
        (d, r, lax.rem(zh + i, n_zh) * n_x + x) for i in sorted({1 % n_zh, n_zh - 1} - {0})
    ]
    near = [(lax.rem(d + i, n_dp), r, c) for i in far_first(n_dp) if i]
    near += [(d, lax.rem(zl + j, n_zl) * 2 + core, c) for j in far_first(n_zl) if j]
    near += [(d, r, zh * n_x + lax.rem(x + j, n_x)) for j in far_first(n_x) if j]
    near += z_near
    contacts = [*near, mate]
    z_peers = [
        (d, lax.rem(zl + j, n_zl) * 2 + core, lax.rem(zh + i, n_zh) * n_x + x)
        for i in far_first(n_zh)
        for j in far_first(n_zl)
        if i or j
    ]
    xy_peers = [
        (lax.rem(d + i, n_dp), r, zh * n_x + lax.rem(x + j, n_x))
        for i in far_first(n_dp)
        for j in far_first(n_x)
        if i or j
    ]
    xzc_peers = [
        (d, zl * 2 + lax.rem(core + k, 2), lax.rem(zh + i, n_zh) * n_x + lax.rem(x + j, n_x))
        for i in far_first(n_zh)
        for j in far_first(n_x)
        for k in range(2)
        if i or j or k
    ]
    xzc_mine = c * 2 + core
    dp_peers = [(lax.rem(d + i, n_dp), r, c) for i in far_first(n_dp) if i]
    z_mine, xy_mine = zh * n_zl + zl, d * n_x + x

    def remote(src, dst, send, recv, to):
        return pltpu.make_async_remote_copy(
            src, dst, send, recv, device_id=to, device_id_type=MESH
        )

    loads = [
        pltpu.make_async_copy(grad.at[0, d], own, loc.at[0]),
        pltpu.make_async_copy(grad.at[0, dn, pl.ds(0, HALF)], next_own, loc.at[1]),
        pltpu.make_async_copy(grad.at[0, dp_, pl.ds(HALF, HALF)], prev_own, loc.at[2]),
        pltpu.make_async_copy(master.at[0], m_buf, loc.at[3]),
        pltpu.make_async_copy(row_prev, rm_buf, loc.at[4]),
        pltpu.make_async_copy(col_prev, cm_buf, loc.at[5]),
        pltpu.make_async_copy(history, old, loc.at[6]),
    ]

    barrier = pltpu.get_barrier_semaphore()
    for p in contacts:
        pl.semaphore_signal(barrier, inc=1, device_id=p, device_id_type=MESH)
    for cp in loads:
        cp.start()
    pl.semaphore_wait(barrier, len(contacts))

    n_half = HALF // CHUNK
    sends = []
    first = []
    for i in range(n_half):
        lo, hi = pl.ds(CHUNK * i, CHUNK), pl.ds(HALF + CHUNK * i, CHUNK)
        here = pl.ds(CHUNK * i, CHUNK)
        a = remote(grad.at[0, do, lo], merge_r.at[here], rs_send.at[i], rs_recv.at[i], right)
        b = remote(grad.at[0, do, hi], merge_l.at[here], rs_send.at[2 + i], rs_recv.at[2 + i], left)
        a.start()
        b.start()
        first.append((a, b))
    plain_r = remote(
        grad.at[0, dn, pl.ds(HALF, HALF)], from_l.at[pl.ds(HALF, HALF)], rs_send.at[4], rs_recv.at[4], right
    )
    plain_l = remote(
        grad.at[0, dp_, pl.ds(0, HALF)], from_r.at[pl.ds(0, HALF)], rs_send.at[5], rs_recv.at[5], left
    )
    plain_r.start()
    plain_l.start()
    for p in near:
        pl.semaphore_signal(greet.at[0], inc=1, device_id=p, device_id_type=MESH)
    loads[3].wait()
    masters[d] = m_buf[pl.ds(LATE, EARLY)].astype(jnp.bfloat16)
    loads[1].wait()
    loads[2].wait()
    merged = []
    for i in range(n_half):
        here, hi = pl.ds(CHUNK * i, CHUNK), pl.ds(HALF + CHUNK * i, CHUNK)
        a, b = first[i]
        a.wait_recv()
        sum_r[here] = (next_own[here].astype(F32) + merge_r[here].astype(F32)).astype(jnp.bfloat16)
        m = remote(sum_r.at[here], from_l.at[here], rs_send.at[6 + i], rs_recv.at[6 + i], right)
        m.start()
        b.wait_recv()
        sum_l[here] = (prev_own[here].astype(F32) + merge_l[here].astype(F32)).astype(jnp.bfloat16)
        n = remote(sum_l.at[here], from_r.at[hi], rs_send.at[8 + i], rs_recv.at[8 + i], left)
        n.start()
        merged.append((m, n))

    pl.semaphore_wait(greet.at[0], len(near))
    for p in z_near:
        pl.semaphore_signal(greet.at[1], inc=1, device_id=p, device_id_type=MESH)
    loads[0].wait()
    plain_r.wait_recv()
    plain_l.wait_recv()
    col_sum = jnp.zeros((8, COLS), F32)
    for i in range(n_half):
        m, n = merged[i]
        for half, cp in ((0, m), (1, n)):
            cp.wait_recv()
            rows = pl.ds(HALF * half + CHUNK * i, CHUNK)
            g = own[rows].astype(F32) + from_l[rows].astype(F32) + from_r[rows].astype(F32)
            g_buf[rows] = g
            square = g * g + epsilon
            for j in range(CHUNK // 8):
                col_sum = col_sum + square[8 * j : 8 * j + 8]
            lanes = square[:, 0:128]
            for k in range(1, TILES):
                lanes = lanes + square[:, 128 * k : 128 * k + 128]
            rowp[rows] = lanes

    flat = jnp.sum(col_sum, axis=0, keepdims=True)
    packed = jnp.concatenate([flat[:, 128 * k : 128 * k + 128] for k in range(TILES)], axis=0)
    core_c[0] = packed
    core_c_copy = remote(core_c.at[0], core_c.at[1], core_send.at[0], core_recv.at[0], mate)
    core_c_copy.start()

    def group_start(buf, mine, peers, i):
        for p in peers:
            remote(buf.at[mine], buf.at[mine], grp_send.at[i], grp_recv.at[i], p).start()

    def group_wait(buf, peers, i):
        whole_wait(buf.at[pl.ds(0, len(peers))], grp_recv.at[i])

    def group_done(buf, peers, i):
        whole_wait(buf.at[pl.ds(0, len(peers))], grp_send.at[i])

    def block_start(buf, i):
        for p in dp_peers:
            remote(buf.at[d], buf.at[d], ag_send.at[i], ag_recv.at[i], p).start()

    def block_wait(i):
        whole_wait(masters.at[pl.ds(0, n_dp - 1)], ag_recv.at[i])

    def block_done(i):
        whole_wait(masters.at[pl.ds(0, n_dp - 1)], ag_send.at[i])

    def add_all(buf, n):
        total = buf[0]
        for k in range(1, n):
            total = total + buf[k]
        return total

    def lanes_to_row(values):
        return jnp.sum(values.T, axis=0, keepdims=True)

    def row_to_lanes(values):
        return jnp.broadcast_to(values, (128, 128)).T

    xz_r[c] = lanes_to_row(rowp[...])
    if z_near:
        pl.semaphore_wait(greet.at[1], len(z_near))
    group_start(xz_r, c, xz_peers, 0)
    pl.semaphore_signal(greet.at[2], inc=1, device_id=mate, device_id_type=MESH)
    core_c_copy.wait_recv()
    yz_c[q] = core_c[0] + core_c[1]
    group_start(yz_c, q, yz_peers, 1)
    block_start(masters, 0)
    loads[4].wait()
    loads[5].wait()
    group_wait(yz_c, yz_peers, 1)
    col_total = add_all(yz_c, n_yz)
    col_old = jnp.concatenate(
        [cm_buf[pl.ds(128 * k, 128)].reshape(1, 128) for k in range(TILES)], axis=0
    )
    col_new = decay_rate * col_old + (1.0 - decay_rate) * (col_total / total_rows)
    for k in range(TILES):
        col_out[pl.ds(128 * k, 128)] = col_new[k]
    inv_col = 1.0 / col_new
    root_col = 1.0 / jnp.sqrt(col_new)

    lanes = jnp.zeros((ROWS, 128), F32)
    for k in range(TILES):
        g = g_buf[:, pl.ds(128 * k, 128)]
        lanes = lanes + g * g * inv_col[k : k + 1]
    pl.semaphore_wait(greet.at[2], 1)
    xz_t[xzc_mine] = lanes_to_row(lanes)
    group_start(xz_t, xzc_mine, xzc_peers, 2)
    group_wait(xz_r, xz_peers, 0)
    row_total = add_all(xz_r, n_col)
    row_new = decay_rate * rm_buf[...] + (1.0 - decay_rate) * (row_total / total_cols)
    row_out[...] = row_new
    core_s[0] = row_new
    core_s_copy = remote(core_s.at[0], core_s.at[1], core_send.at[1], core_recv.at[1], mate)
    core_s_copy.start()
    row_factor = row_to_lanes(1.0 / jnp.sqrt(row_new))
    for k in range(TILES):
        cols = pl.ds(128 * k, 128)
        step = g_buf[:, cols] * row_factor * root_col[k : k + 1]
        g_buf[:, cols] = step
        steps[d, :, cols] = step[LATE:].astype(jnp.bfloat16)
    block_start(steps, 1)
    core_s_copy.wait_recv()
    row_first = jnp.where(core == 0, row_new, core_s[1])
    row_second = jnp.where(core == 0, core_s[1], row_new)
    group_wait(xz_t, xzc_peers, 2)
    first_total, second_total = xz_t[0], xz_t[1]
    for k in range(1, n_col):
        first_total = first_total + xz_t[2 * k]
        second_total = second_total + xz_t[2 * k + 1]
    weighted = first_total / row_first + second_total / row_second

    yz_s[q] = jnp.concatenate([weighted, row_first + row_second], axis=0)
    group_start(yz_s, q, yz_peers, 3)
    loads[6].wait()
    largest_old = old[0]
    for i in range(1, 16):
        largest_old = jnp.maximum(largest_old, old[i])
    lane = lax.broadcasted_iota(jnp.int32, (1, 128), 1)
    shifted = jnp.zeros((1, 128), F32)
    for i in range(15):
        shifted = jnp.where(lane == i, old[i + 1], shifted)
    scale = code_limit / jnp.full((1, 128), largest_old, F32)
    group_wait(yz_s, yz_peers, 3)
    totals = jnp.sum(add_all(yz_s, n_yz), axis=1, keepdims=True)
    row_mean = totals[1:2] / total_rows
    step_rms = jnp.sqrt(row_mean * totals[0:1] / (float(total_rows) * float(total_cols)))
    factor = jnp.sqrt(row_mean) / jnp.maximum(1.0, step_rms / clip_limit)
    tail_out[1:2] = jnp.broadcast_to(row_mean, (1, 128))
    tail_out[2:8] = jnp.zeros((6, 128), F32)

    rate = learn_rate * factor
    largest = jnp.zeros((ROWS, 128), F32)
    for k in range(TILES):
        cols = pl.ds(128 * k, 128)
        largest = jnp.maximum(largest, jnp.abs(m_buf[:, cols] - rate * g_buf[:, cols]))
    core_m[0] = jnp.max(largest, axis=0, keepdims=True)
    core_m_copy = remote(core_m.at[0], core_m.at[1], core_send.at[2], core_recv.at[2], mate)
    core_m_copy.start()
    for k in range(TILES):
        cols = pl.ds(128 * k, 128)
        update = g_buf[:, cols] * factor
        up_out[:, cols] = update
        nm_out[:, cols] = m_buf[:, cols] - learn_rate * update
    core_m_copy.wait_recv()
    z_m[z_mine] = jnp.maximum(core_m[0], core_m[1])
    group_start(z_m, z_mine, z_peers, 4)

    top, bottom = pl.ds(0, LATE // 2), pl.ds(LATE // 2, LATE // 2)
    codes_out[d, pl.ds(0, LATE)] = jnp.clip(nm_out[pl.ds(0, LATE)] * scale[:, 0:1], -code_limit, code_limit).astype(
        jnp.bfloat16
    )
    to_right = [
        remote(codes_out.at[d, part], codes_out.at[d, part], ag_send.at[2 + i], ag_recv.at[2 + i], right)
        for i, part in enumerate((top, bottom))
    ]
    to_left = [
        remote(codes_out.at[d, part], codes_out.at[d, part], ag_send.at[4 + i], ag_recv.at[4 + i], left)
        for i, part in enumerate((bottom, top))
    ]
    for i in range(2):
        to_right[i].start()
        to_left[i].start()

    to_right[0].wait_recv()
    on_right = remote(
        codes_out.at[dp_, top], codes_out.at[dp_, top], ag_send.at[6], ag_recv.at[6], right
    )
    on_right.start()
    to_left[0].wait_recv()
    on_left = remote(
        codes_out.at[dn, bottom], codes_out.at[dn, bottom], ag_send.at[7], ag_recv.at[7], left
    )
    on_left.start()

    def max_all(buf, n):
        total = buf[0]
        for k in range(1, n):
            total = jnp.maximum(total, buf[k])
        return total

    group_wait(z_m, z_peers, 4)
    xy_m[xy_mine] = max_all(z_m, len(z_peers) + 1)
    group_start(xy_m, xy_mine, xy_peers, 5)

    block_wait(0)
    block_wait(1)
    for j in range(n_dp):
        moved = masters[j].astype(F32) - rate * steps[j].astype(F32)
        codes_out[j, pl.ds(LATE, EARLY)] = jnp.clip(moved * scale[:, 0:1], -code_limit, code_limit).astype(jnp.bfloat16)

    for a, b in first:
        a.wait_send()
        b.wait_send()
    plain_r.wait_send()
    plain_l.wait_send()
    for m, n in merged:
        m.wait_send()
        n.wait_send()
    core_c_copy.wait_send()
    core_s_copy.wait_send()
    core_m_copy.wait_send()
    group_done(xz_r, xz_peers, 0)
    group_done(yz_c, yz_peers, 1)
    group_done(xz_t, xzc_peers, 2)
    group_done(yz_s, yz_peers, 3)
    group_done(z_m, z_peers, 4)
    to_right[1].wait_recv()
    to_left[1].wait_recv()
    on_right.wait_recv()
    on_left.wait_recv()
    group_wait(xy_m, xy_peers, 5)
    newest = jnp.max(max_all(xy_m, len(xy_peers) + 1), axis=1, keepdims=True)
    tail_out[0:1] = jnp.where(lane == 15, newest, shifted)
    for cp in (*to_right, *to_left, on_right, on_left):
        cp.wait_send()
    block_done(0)
    block_done(1)
    group_done(xy_m, xy_peers, 5)


def finish_kernel(
    nm_in, up_in, codes_in, row_in, col_in, tail,
    nm_out, up_out, row_out, col_out, codes_out, history_out, mean_out, last, mean, sems,
):
    copies = [
        pltpu.make_async_copy(a, b, sems.at[i])
        for i, (a, b) in enumerate(
            (
                (codes_in, codes_out),
                (nm_in, nm_out),
                (up_in, up_out),
                (row_in, row_out),
                (col_in, col_out),
                (last, history_out),
                (mean, mean_out),
            )
        )
    ]
    for cp in copies[:5]:
        cp.start()
    last[...] = tail[0, 0:16]
    mean[...] = tail[1, 0:1]
    for cp in copies[5:]:
        cp.start()
    for cp in copies:
        cp.wait()


def body(sizes, grad, master, row_prev, col_prev, history):
    n_dp, n_row, n_col = sizes
    n_yz = n_dp * n_row // 2
    n_x = min(n_col, 4)
    bf = jnp.bfloat16
    anywhere = pl.BlockSpec(memory_space=pl.ANY)
    vmem = pl.BlockSpec(memory_space=pltpu.VMEM)
    hbm = pl.BlockSpec(memory_space=pltpu.HBM)
    block = jax.ShapeDtypeStruct((ROWS, COLS), F32)
    codes = jax.ShapeDtypeStruct((n_dp, ROWS, COLS), bf)
    V = pltpu.VMEM
    dma = pltpu.SemaphoreType.DMA
    row_like, col_like = jax.ShapeDtypeStruct((1, ROWS), F32), jax.ShapeDtypeStruct((COLS,), F32)
    given = [pltpu.with_memory_space_constraint(a, pltpu.HBM) for a in (grad, master, row_prev, col_prev, history)]
    new_master, update, coded, row_new, col_new, tail = pl.pallas_call(
        functools.partial(step_kernel, sizes),
        out_shape=[block, block, codes, row_like, col_like, jax.ShapeDtypeStruct((8, 128), F32)],
        in_specs=[hbm] * 5,
        out_specs=[vmem] * 6,
        scratch_shapes=[
            V((HALF, COLS), bf), V((HALF, COLS), bf),
            V((ROWS, COLS), bf), V((ROWS, COLS), bf), V((ROWS, COLS), bf),
            V((HALF, COLS), bf), V((HALF, COLS), bf), V((HALF, COLS), bf), V((HALF, COLS), bf),
            V((ROWS, COLS), F32), V((ROWS, COLS), F32), V((ROWS, 128), F32), V((1, 128), F32), V((COLS,), F32), pltpu.SMEM((16,), F32),
            V((2, 8, 128), F32), V((n_yz, 8, 128), F32),
            V((n_col, 1, 128), F32), V((2 * n_col, 1, 128), F32),
            V((2, 1, 128), F32), V((n_yz, 2, 128), F32),
            V((n_col // n_x * n_row // 2, 1, 128), F32), V((2, 1, 128), F32), V((n_dp * n_x, 1, 128), F32),
            dma((10,)), dma((10,)), dma((8,)), dma((3,)), dma((3,)), dma((6,)), dma((6,)), dma((8,)), dma((8,)),
            pltpu.SemaphoreType.REGULAR((3,)), V((n_dp, EARLY, COLS), bf), V((n_dp, EARLY, COLS), bf),
        ],
        compiler_params=pltpu.CompilerParams(
            collective_id=0, has_side_effects=True, vmem_limit_bytes=16 * 1024 * 1024
        ),
        name="step",
    )(*given)
    new_master, update, row_new, col_new, coded, new_history, row_mean = pl.pallas_call(
        finish_kernel,
        out_shape=[
            block, block, row_like, col_like, codes,
            jax.ShapeDtypeStruct((16,), F32), jax.ShapeDtypeStruct((1,), F32),
        ],
        in_specs=[anywhere] * 5 + [vmem],
        out_specs=[hbm] * 7,
        scratch_shapes=[V((16,), F32), V((1,), F32), dma((7,))],
        compiler_params=pltpu.CompilerParams(vmem_limit_bytes=1024 * 1024),
        name="finish",
    )(new_master, update, coded, row_new, col_new, tail)
    return (
        new_master[None], update[None], row_new, col_new, coded, new_history, row_mean.reshape(()),
    )


def solution(mesh):
    sizes = tuple(mesh.shape[a] for a in ("dp", "row", "col"))
    placed = (P("dp", None, "row", "col"), P("dp", "row", "col"), P("dp", "row"), P("col"), P())
    return jax.shard_map(
        functools.partial(body, sizes),
        mesh=mesh,
        in_specs=placed,
        out_specs=(
            P("dp", "row", "col"),
            P("dp", "row", "col"),
            P("dp", "row"),
            P("col"),
            P(None, "row", "col"),
            P(),
            P(),
        ),
        check_vma=False,
    )
```
